512 devices in a mesh: shard: 128 (over z, y, core), tile: 4 (over x).
Axes of the slice: x: 4, y: 8, z: 8, core: 2. Of those that a mesh axis runs over, the one named last changes fastest.
Arguments:
- embeddings: bfloat16 [262144, 768], P(('shard', 'tile'))
- cluster: int32 [262144], P(('shard', 'tile')), may hold values from 0 to 15
- home: int32 [262144], P(('shard', 'tile')), may hold values from 0 to 127, as said below
Outputs:
- density: float32 [262144], P(('shard', 'tile'))
The draws below stay inside these ranges and needn't reach their ends.
Inputs may be any that keep to these rules, and one draw needn't show every extreme that they name: `home`: among the rows of one device at most 8 name one owner, and in every draw some owner is named exactly that often by the rows of every device.
All inputs are finite; a program needn't handle non-finite values.
Results may differ from the reference program's by a relative error of at most 0.0045.
Values may be sent and summed in bfloat16 or wider, within the bound.
A program may use at most 64 MiB of HBM per device.

```python
import math
import jax
import jax.numpy as jnp
import numpy as np
from jax import lax

D = 768
ROWS_DEV = 512
CLUS_OWN = 16
N_SHARD = 128
N_TILE = 4


def routing(key):
    subkeys = jax.random.split(key, 5)
    sources = N_SHARD * N_TILE
    capacity = 2 * ROWS_DEV // N_SHARD
    chosen = jax.random.permutation(subkeys[0], N_SHARD)[:N_SHARD // 8]
    popular = jnp.zeros((N_SHARD,), jnp.int32).at[chosen].set(1)
    noise_int = jax.random.randint(subkeys[1], (sources, N_SHARD), 0, 2 ** 20)
    scoring = popular[None, :] * 2 ** 30 + noise_int * N_SHARD + jnp.arange(N_SHARD, dtype=jnp.int32)[None, :]
    picked = lax.top_k(scoring, N_SHARD // 2)[1].astype(jnp.int32)
    targets = jnp.repeat(picked, capacity, axis=1)
    shuffle_int = jax.random.randint(subkeys[2], (sources, ROWS_DEV), 0, 2 ** 18) * ROWS_DEV + jnp.arange(ROWS_DEV, dtype=jnp.int32)[None, :]
    shuffled = jnp.argsort(shuffle_int, axis=1)
    home = jnp.take_along_axis(targets, shuffled, axis=1).reshape(-1).astype(jnp.int32)
    weights = 2.0 ** (-np.arange(CLUS_OWN) / 2.0)
    cumulative = np.cumsum(weights) / weights.sum()
    thresholds = jnp.asarray((cumulative[:-1] * 65536.0).astype(np.int32))
    uniform_int = jax.random.randint(subkeys[3], (sources * ROWS_DEV,), 0, 65536)
    rank_local = jnp.sum((uniform_int[:, None] >= thresholds[None, :]).astype(jnp.int32), axis=1)
    relabel_int = jax.random.randint(subkeys[4], (N_SHARD, CLUS_OWN), 0, 2 ** 20) * CLUS_OWN + jnp.arange(CLUS_OWN, dtype=jnp.int32)[None, :]
    relabel = jnp.argsort(relabel_int, axis=1).astype(jnp.int32)
    cluster = relabel[home, rank_local]
    return (home, cluster)


def draw_home(key, part):
    return routing(key)[0]


def draw_cluster(key, part):
    return routing(key)[1]


def draw_embeddings(key, part):
    home, cluster = routing(key)
    key = jax.random.fold_in(key, 11)
    subkeys = jax.random.split(key, 9)
    row_count = home.shape[0]
    labels = home * CLUS_OWN + cluster
    branches = 32
    centers = jax.random.normal(subkeys[0], (N_SHARD * CLUS_OWN, D), jnp.float32)
    branch_index = jax.random.randint(subkeys[1], (row_count,), 0, branches)
    branch_label = labels * branches + branch_index

    def branch_vector(label_value):
        return jax.random.normal(jax.random.fold_in(subkeys[2], label_value), (D,), jnp.float32)
    branch_vectors = jax.vmap(branch_vector)(branch_label)
    center_pull = jnp.exp(jax.random.uniform(subkeys[3], (row_count, 1), jnp.float32, math.log(0.3), math.log(1.5)))
    branch_pull = jnp.exp(jax.random.uniform(subkeys[4], (row_count, 1), jnp.float32, math.log(0.6), math.log(2.5)))
    scaling = jnp.exp(jax.random.uniform(subkeys[5], (row_count, 1), jnp.float32, 0.0, math.log(10.0)))
    closeness = jnp.exp(jax.random.uniform(subkeys[6], (row_count, 1), jnp.float32, math.log(0.14), math.log(0.48)))
    noise = jax.random.normal(subkeys[7], (row_count, D), jnp.float32)
    jitter = jax.random.normal(subkeys[8], (row_count, D), jnp.float32)
    shared = jnp.zeros((1, D), jnp.float32)
    anchored = center_pull * centers[labels] + branch_pull * branch_vectors + noise + shared
    expected = jnp.sqrt(1.0 + center_pull * center_pull + branch_pull * branch_pull)
    ordering = jnp.argsort(labels, stable=True).astype(jnp.int32)
    rank_sorted = jnp.zeros((row_count,), jnp.int32).at[ordering].set(jnp.arange(row_count, dtype=jnp.int32))
    previous = ordering[jnp.maximum(rank_sorted - 1, 0)]
    same_label = (rank_sorted > 0) & (labels[previous] == labels)
    flagged = jax.random.randint(jax.random.fold_in(subkeys[1], 5), (row_count,), 0, 100) < 15
    copier = flagged & same_label & jnp.logical_not(flagged[previous])
    copies = anchored[previous] + closeness * expected[previous] * jitter
    values = scaling * jnp.where(copier[:, None], copies, anchored)
    return values.astype(jnp.bfloat16)


def setup_inputs(seed: int = 0) -> dict:
    arg_keys = jax.random.split(jax.random.key(seed), 4)
    return {
        "embeddings": draw_embeddings(jax.random.fold_in(arg_keys[3], 71), 0),
        "cluster": draw_cluster(jax.random.fold_in(arg_keys[3], 71), 0),
        "home": draw_home(jax.random.fold_in(arg_keys[3], 71), 0),
    }


def reference(embeddings, cluster, home):
    values = embeddings.astype(jnp.float32)
    unit_rows = (values * lax.rsqrt(lax.optimization_barrier(jnp.sum(values * values, axis=1, keepdims=True)) + 1e-06)).astype(jnp.bfloat16)
    row_count = values.shape[0]
    feature_count = values.shape[1]
    labels = home * CLUS_OWN + cluster
    ordering = jnp.argsort(labels, stable=True).astype(jnp.int32)
    tallies = jnp.zeros((N_SHARD,), jnp.int32).at[home].add(1)
    offsets = jnp.cumsum(tallies) - tallies
    sorted_home = home[ordering]
    position = jnp.arange(row_count, dtype=jnp.int32) - offsets[sorted_home]
    capacity = N_TILE * 2 * ROWS_DEV
    layout = jnp.full((N_SHARD, capacity), row_count, jnp.int32).at[sorted_home, position].set(ordering)
    unit_pad = jnp.concatenate([unit_rows, jnp.zeros((1, feature_count), jnp.bfloat16)], axis=0)
    label_pad = jnp.concatenate([labels, jnp.full((1,), -1, jnp.int32)], axis=0)
    block = math.gcd(512, capacity)
    blocks = capacity // block

    def per_owner(index_row):
        query_rows = unit_pad[index_row]
        row_labels = label_pad[index_row]
        filled = row_labels >= 0
        lowest = jnp.where(filled, row_labels, 2 ** 30).reshape(blocks, block).min(axis=1)
        highest = jnp.where(filled, row_labels, -1).reshape(blocks, block).max(axis=1)
        pieces = []
        for row_block in range(blocks):
            query_part = query_rows[row_block * block:(row_block + 1) * block]
            query_labels = row_labels[row_block * block:(row_block + 1) * block]
            running = jnp.zeros((block,), jnp.float32)
            for col_block in range(blocks):
                key_part = query_rows[col_block * block:(col_block + 1) * block]
                key_labels = row_labels[col_block * block:(col_block + 1) * block]

                def compute(query_part=query_part, query_labels=query_labels, key_part=key_part, key_labels=key_labels):
                    scores = jnp.dot(query_part, key_part.T, preferred_element_type=jnp.float32)
                    matched = (query_labels[:, None] == key_labels[None, :]) & (query_labels[:, None] >= 0)
                    return lax.optimization_barrier(jnp.sum(jnp.where(matched, jnp.exp((scores - 1.0) * 10.0), 0.0), axis=1))

                def nothing():
                    return jnp.zeros((block,), jnp.float32)
                touching = (lowest[row_block] <= highest[col_block]) & (lowest[col_block] <= highest[row_block])
                running = running + lax.cond(touching, compute, nothing)
            pieces.append(running)
        return jnp.concatenate(pieces)
    results = lax.map(per_owner, layout)
    density = jnp.zeros((row_count + 1,), jnp.float32).at[layout.reshape(-1)].set(results.reshape(-1))
    return density[:row_count]
```

```python
import functools

import jax
import jax.numpy as jnp
from jax import lax
from jax.experimental import pallas as pl
from jax.experimental.pallas import tpu as pltpu
from jax.sharding import PartitionSpec as P

F32 = jnp.float32
BF16 = jnp.bfloat16
I32 = jnp.int32
MESH = pl.DeviceIdType.MESH
CAP = 8
SCALE = 10.0 * 1.4426950408889634


def iota(shape, dim):
    return lax.broadcasted_iota(I32, shape, dim)


def nt_dot(left, right):
    return lax.dot_general(left, right, (((1,), (1,)), ((), ())), preferred_element_type=F32)


def kernel(
    na, nx, home_ref, cluster_ref, emb_ref, out_ref,
    unit, out1, in1, in2, own, sib, acc,
    ids1, ids1_in, ids2, ids2_in, key_ids, sib_ids, query_ids,
    den, den_in, ret, ret_in,
    send1, recv1, send2, recv2, send3, recv3,
    isend1, irecv1, isend2, irecv2, isend3, irecv3,
    dsend1, drecv1, dsend2, drecv2, local,
):
    nb = na
    nk = 2 * nb // nx
    half = nx // 2
    rows, feat = emb_ref.shape
    hf = feat // 2
    chunk = nb * nx * CAP
    wide = nx * CAP
    per_step = nx * nk * CAP
    lanes = 128

    shard = lax.axis_index("shard")
    x = lax.axis_index("tile")
    core = shard % 2
    y = (shard // 2) % nb
    z = shard // (2 * nb)
    a = z + core * (y - z)
    b = y + core * (z - y)

    def dev(a_to, b_to, x_to):
        z_to = a_to + core * (b_to - a_to)
        y_to = b_to + core * (a_to - b_to)
        return ((z_to * nb + y_to) * 2 + core, x_to)

    sibling = (shard + 1 - 2 * core, x)

    def delta(t):
        return ((t + 1) // 2) * (2 * (t % 2) - 1) + na

    def a_dst(t):
        return (a + delta(t)) % na

    def a_src(t):
        return (a - delta(t) + 2 * na) % na

    def b_dst(k):
        c_to = k // (nb // nx)
        return (x - a - half * c_to + 2 * nx + na * nx) % nx + nx * (k % (nb // nx))

    turn = (x - a - b + 2 * na * nx) % nx
    computes = turn % half == 0
    k_self = (turn // half) * (nb // nx) + b // nx

    barrier = pltpu.get_barrier_semaphore()

    def greet_a(i, carry):
        t, xs = i // nx, i % nx

        @pl.when(i != x)
        def _():
            pl.semaphore_signal(barrier, inc=1, device_id=dev(a_dst(t), b, xs), device_id_type=MESH)
        return carry

    lax.fori_loop(0, na * nx, greet_a, 0)

    def greet_b(i, carry):
        @pl.when(i != b)
        def _():
            pl.semaphore_signal(barrier, inc=1, device_id=dev(a, i, x), device_id_type=MESH)
        return carry

    lax.fori_loop(0, nb, greet_b, 0)
    pl.semaphore_signal(barrier, inc=1, device_id=sibling, device_id_type=MESH)

    home = home_ref[...]
    named = iota((2 * na * nb, rows), 0) == home
    before = (iota((rows, rows), 0) < iota((rows, rows), 1)).astype(BF16)
    counts = jnp.dot(named.astype(BF16), before, preferred_element_type=F32)
    pos = jnp.sum(jnp.where(named, counts, 0.0), axis=0, keepdims=True).astype(I32)
    c_own = home % 2
    y_own = (home // 2) % nb
    z_own = home // (2 * nb)
    a_own = z_own + core * (y_own - z_own)
    b_own = y_own + core * (z_own - y_own)
    x_own = (a_own + b_own + half * c_own) % nx
    k_own = c_own * (nb // nx) + b_own // nx
    step = (a_own - a + na) % na
    step = jnp.where(step <= na // 2, jnp.maximum(2 * step - 1, 0), 2 * (na - step))
    message = step * nx + x_own
    lane = k_own * CAP + pos
    slot = message * (nk * CAP) + lane

    marks = (cluster_ref[...] + 1).astype(F32)
    in_message = (iota((na * nx, rows), 0) == message).astype(BF16)
    in_lane = jnp.where(iota((lanes, rows), 0) == lane, marks, 0.0).astype(BF16)
    tags = nt_dot(in_message, in_lane)
    for m in range(na * nx):
        ids1[m] = tags[m : m + 1]

    values = emb_ref[...].astype(F32)
    unit[...] = (
        values * lax.rsqrt(jnp.sum(values * values, axis=1, keepdims=True) + 1e-06)
    ).astype(BF16)

    pl.semaphore_wait(barrier, na * nx - 1 + nb - 1 + 1)

    def ids1_copy(t, xs):
        return pltpu.make_async_remote_copy(
            src_ref=ids1.at[t * nx + xs], dst_ref=ids1_in.at[t * nx + x],
            send_sem=isend1.at[t, xs], recv_sem=irecv1,
            device_id=dev(a_dst(t), b, xs), device_id_type=MESH,
        )

    def out1_copy(t, xs):
        return pltpu.make_async_remote_copy(
            src_ref=out1.at[t, xs], dst_ref=in1.at[t, x],
            send_sem=send1.at[t, xs], recv_sem=recv1.at[t],
            device_id=dev(a_dst(t), b, xs), device_id_type=MESH,
        )

    def ids1_send(i, carry):
        t, xs = i // nx, i % nx

        @pl.when(i != x)
        def _():
            ids1_copy(t, xs).start()

        @pl.when(i == x)
        def _():
            pltpu.make_async_copy(ids1.at[x], ids1_in.at[x], irecv1).start()
        return carry

    lax.fori_loop(0, na * nx, ids1_send, 0)

    def place(t, carry):
        pick = (iota((per_step, rows), 0) + t * per_step == slot).astype(BF16)
        placed = jnp.dot(pick, unit[...], preferred_element_type=F32)
        placed = placed.reshape(nx * nk, CAP, feat)
        placed = jnp.concatenate([placed[:, :, :hf], placed[:, :, hf:]], axis=1).astype(BF16)
        out1[t] = placed.reshape(nx, nk, 2 * CAP, hf)
        for xs in range(nx):
            @pl.when((t > 0) | (xs != x))
            def _():
                out1_copy(t, xs).start()

            @pl.when((t == 0) & (xs == x))
            def _():
                pltpu.make_async_copy(out1.at[0, x], in1.at[0, x], recv1.at[0]).start()
        return carry

    lax.fori_loop(0, na, place, 0)

    pltpu.make_async_copy(ids1, ids1_in, irecv1).wait()
    tags_in = [
        jnp.concatenate([ids1_in[t * nx + xs] for t in range(na)], axis=0) for xs in range(nx)
    ]
    at_lane = iota((na, lanes), 1)

    def shifted(block, source, target):
        kept = jnp.where((at_lane >= source * CAP) & (at_lane < source * CAP + CAP), block, 0.0)
        turns = ((target - source) * CAP) % lanes
        return pltpu.roll(kept, turns, 1) if turns else kept

    for k in range(nk):
        ids2[k] = functools.reduce(jnp.add, [shifted(tags_in[xs], k, xs) for xs in range(nx)])

    def ids2_copy(k):
        return pltpu.make_async_remote_copy(
            src_ref=ids2.at[k], dst_ref=ids2_in.at[b],
            send_sem=isend2.at[k], recv_sem=irecv2,
            device_id=dev(a, b_dst(k), x), device_id_type=MESH,
        )

    def rows2_copy(t, k):
        return pltpu.make_async_remote_copy(
            src_ref=in1.at[t, :, k], dst_ref=in2.at[t, b],
            send_sem=send2.at[t, k], recv_sem=recv2.at[t],
            device_id=dev(a, b_dst(k), x), device_id_type=MESH,
        )

    for k in range(nk):
        @pl.when(b_dst(k) != b)
        def _():
            ids2_copy(k).start()

        @pl.when(b_dst(k) == b)
        def _():
            pltpu.make_async_copy(ids2.at[k], ids2_in.at[b], irecv2).start()

    def sib_ids_copy():
        return pltpu.make_async_remote_copy(
            src_ref=key_ids, dst_ref=sib_ids, send_sem=isend3, recv_sem=irecv3,
            device_id=sibling, device_id_type=MESH,
        )

    def sib_rows_copy(t):
        return pltpu.make_async_remote_copy(
            src_ref=own.at[t], dst_ref=sib.at[t], send_sem=send3.at[t], recv_sem=recv3.at[t],
            device_id=sibling, device_id_type=MESH,
        )

    def spread_ids():
        pltpu.make_async_copy(ids2_in, ids2_in, irecv2).wait()
        same = iota((chunk, lanes), 1) == iota((chunk, lanes), 0) % wide
        for t in range(na):
            block = jnp.concatenate(
                [jnp.broadcast_to(ids2_in[j, t : t + 1, :], (wide, lanes)) for j in range(nb)],
                axis=0,
            )
            block = jnp.where(same, block, 0.0)
            query_ids[t] = jnp.broadcast_to(
                jnp.sum(block, axis=1, keepdims=True), (chunk, lanes)
            )
            key_ids[t] = nt_dot(jnp.ones((8, lanes), BF16), block.astype(BF16))
        sib_ids_copy().start()
        acc[...] = jnp.zeros_like(acc)

    def add_pairs(q, keys, ids, t):
        scores = nt_dot(own[q], keys[t])
        weights = jnp.exp2(scores * SCALE)
        mine = query_ids[q]
        theirs = ids[t, 0:1, :]
        total = acc[q]
        for j in range(0, chunk, lanes):
            total += jnp.where(mine == theirs[:, j : j + lanes], weights[:, j : j + lanes], 0.0)
        acc[q] = total

    def pair_sums(t, carry):
        pltpu.make_async_copy(in2.at[t], in2.at[t], recv2.at[t]).wait()
        block = in2[t].reshape(nb * nx, 2 * CAP, hf).astype(F32)
        block = jnp.concatenate([block[:, :CAP, :], block[:, CAP:, :]], axis=2)
        own[t] = block.reshape(chunk, feat).astype(BF16)
        sib_rows_copy(t).start()

        def own_pairs(i, c):
            fresh = i <= t
            add_pairs(jnp.where(fresh, i, t), own, key_ids, jnp.where(fresh, t, i - t - 1))
            return c

        lax.fori_loop(0, 2 * t + 1, own_pairs, 0)
        sib_rows_copy(t).wait_recv()

        def sib_pairs(i, c):
            fresh = i <= t
            add_pairs(jnp.where(fresh, i, t), sib, sib_ids, jnp.where(fresh, t, i - t - 1))
            return c

        lax.fori_loop(0, 2 * t + 1, sib_pairs, 0)
        return carry

    def forward(t, carry):
        pltpu.make_async_copy(in1.at[t], in1.at[t], recv1.at[t]).wait()
        for k in range(nk):
            @pl.when(b_dst(k) != b)
            def _():
                rows2_copy(t, k).start()

            @pl.when(b_dst(k) == b)
            def _():
                pltpu.make_async_copy(in1.at[t, :, k], in2.at[t, b], recv2.at[t]).start()

        @pl.when(computes & (t == 0))
        def _():
            spread_ids()
            sib_ids_copy().wait_recv()

        @pl.when(computes & (t > 0))
        def _():
            pair_sums(t - 1, 0)
        return carry

    lax.fori_loop(0, na, forward, 0)

    def den1_copy(to):
        return pltpu.make_async_remote_copy(
            src_ref=den.at[to], dst_ref=den_in.at[k_self],
            send_sem=dsend1.at[to], recv_sem=drecv1,
            device_id=dev(a, to, x), device_id_type=MESH,
        )

    @pl.when(computes)
    def _():
        pair_sums(na - 1, 0)
        same = iota((chunk, lanes), 1) == iota((chunk, lanes), 0) % wide
        for t in range(na):
            sums = jnp.sum(acc[t], axis=1, keepdims=True) * (2.0 ** (-SCALE))
            block = jnp.where(same, sums, 0.0).reshape(nb, wide, lanes)
            block = jnp.sum(block, axis=1)
            for j in range(nb):
                den[j, t : t + 1, :] = block[j : j + 1]

        def den1_send(to, carry):
            @pl.when(to != b)
            def _():
                den1_copy(to).start()

            @pl.when(to == b)
            def _():
                pltpu.make_async_copy(den.at[b], den_in.at[k_self], drecv1).start()
            return carry

        lax.fori_loop(0, nb, den1_send, 0)

    pltpu.make_async_copy(den_in, den_in, drecv1).wait()
    for xs in range(nx):
        block = functools.reduce(jnp.add, [shifted(den_in[k], xs, k) for k in range(nk)])
        for t in range(na):
            ret[t * nx + xs] = block[t : t + 1]

    def ret_copy(t, xs):
        return pltpu.make_async_remote_copy(
            src_ref=ret.at[t * nx + xs], dst_ref=ret_in.at[t * nx + x],
            send_sem=dsend2.at[t, xs], recv_sem=drecv2,
            device_id=dev(a_src(t), b, xs), device_id_type=MESH,
        )

    def ret_send(i, carry):
        t, xs = i // nx, i % nx

        @pl.when(i != x)
        def _():
            ret_copy(t, xs).start()

        @pl.when(i == x)
        def _():
            pltpu.make_async_copy(ret.at[x], ret_in.at[x], drecv2).start()
        return carry

    lax.fori_loop(0, na * nx, ret_send, 0)
    pltpu.make_async_copy(ret, ret_in, drecv2).wait()

    table = jnp.concatenate(
        [ret_in[m] for m in range(na * nx)] + [jnp.zeros((lanes - na * nx, lanes), F32)], axis=0
    )
    table = table.T[: nk * CAP]
    chosen = (iota((lanes, rows), 0) == message).astype(BF16)
    high = table.astype(BF16)
    rest = table - high.astype(F32)
    mid = rest.astype(BF16)
    low = (rest - mid.astype(F32)).astype(BF16)
    picked = (
        jnp.dot(low, chosen, preferred_element_type=F32)
        + jnp.dot(mid, chosen, preferred_element_type=F32)
    ) + jnp.dot(high, chosen, preferred_element_type=F32)
    out_ref[...] = jnp.sum(
        jnp.where(iota((nk * CAP, rows), 0) == lane, picked, 0.0), axis=0, keepdims=True
    )

    def drain_a(i, carry):
        t, xs = i // nx, i % nx

        @pl.when(i != x)
        def _():
            ids1_copy(t, xs).wait_send()
            out1_copy(t, xs).wait_send()
            ret_copy(t, xs).wait_send()
        return carry

    lax.fori_loop(0, na * nx, drain_a, 0)
    for k in range(nk):
        @pl.when(b_dst(k) != b)
        def _():
            ids2_copy(k).wait_send()

            def drain_b(t, carry):
                rows2_copy(t, k).wait_send()
                return carry

            lax.fori_loop(0, na, drain_b, 0)

    @pl.when(computes)
    def _():
        sib_ids_copy().wait_send()

        def drain_c(t, carry):
            sib_rows_copy(t).wait_send()

            @pl.when(t != b)
            def _():
                den1_copy(t).wait_send()
            return carry

        lax.fori_loop(0, na, drain_c, 0)


def shards(n_tile, embeddings, cluster, home):
    n_shard = lax.axis_size("shard")
    na = next(n for n in range(1, n_shard + 1) if 2 * n * n == n_shard)
    nx = n_tile
    nk = 2 * na // nx
    rows, feat = embeddings.shape
    chunk = na * nx * CAP
    hf = feat // 2
    messages = na * nx
    vmem = pltpu.VMEM
    dma = pltpu.SemaphoreType.DMA
    out = pl.pallas_call(
        functools.partial(kernel, na, nx),
        out_shape=jax.ShapeDtypeStruct((1, rows), F32),
        in_specs=[pl.BlockSpec(memory_space=pltpu.VMEM)] * 3,
        out_specs=pl.BlockSpec(memory_space=pltpu.VMEM),
        scratch_shapes=[
            vmem((rows, feat), BF16),
            vmem((na, nx, nk, 2 * CAP, hf), BF16),
            vmem((na, nx, nk, 2 * CAP, hf), BF16),
            vmem((na, na, nx, 2 * CAP, hf), BF16),
            vmem((na, chunk, feat), BF16),
            vmem((na, chunk, feat), BF16),
            vmem((na, chunk, 128), F32),
            vmem((messages, 1, 128), F32),
            vmem((messages, 1, 128), F32),
            vmem((nk, na, 128), F32),
            vmem((na, na, 128), F32),
            vmem((na, 8, chunk), F32),
            vmem((na, 8, chunk), F32),
            vmem((na, chunk, 128), F32),
            vmem((na, na, 128), F32),
            vmem((nk, na, 128), F32),
            vmem((messages, 1, 128), F32),
            vmem((messages, 1, 128), F32),
            dma((na, nx)), dma((na,)), dma((na, nk)), dma((na,)), dma((na,)), dma((na,)),
            dma((na, nx)), dma(()), dma((nk,)), dma(()), dma(()), dma(()),
            dma((na,)), dma(()), dma((na, nx)), dma(()), dma(()),
        ],
        compiler_params=pltpu.CompilerParams(
            collective_id=0, has_side_effects=True, vmem_limit_bytes=48 * 2**20
        ),
    )(home.reshape(1, rows), cluster.reshape(1, rows), embeddings)
    return out.reshape(rows)


def solution(mesh):
    return jax.shard_map(
        functools.partial(shards, mesh.shape["tile"]),
        mesh=mesh,
        in_specs=(P(("shard", "tile"), None), P(("shard", "tile")), P(("shard", "tile"))),
        out_specs=P(("shard", "tile")),
        check_vma=False,
    )
```

```python
import functools

import jax
import jax.numpy as jnp
from jax import lax
from jax.experimental import pallas as pl
from jax.experimental.pallas import tpu as pltpu
from jax.sharding import PartitionSpec as P

F32 = jnp.float32
BF16 = jnp.bfloat16
I32 = jnp.int32
MESH = pl.DeviceIdType.MESH
CAP = 8
SCALE = 10.0 * 1.4426950408889634


def iota(shape, dim):
    return lax.broadcasted_iota(I32, shape, dim)


def nt_dot(left, right):
    return lax.dot_general(left, right, (((1,), (1,)), ((), ())), preferred_element_type=F32)


def kernel(
    na, nx, home_hbm, cluster_hbm, emb_hbm, out_ref,
    home_ref, cluster_ref, emb_ref, unit, out1, in1, in2, sib_in, kept, acc, col,
    ids1, ids1_in, ids2, ids2_in, ids2_sib, key_ids, row_ids,
    den, den_in, ret, ret_in,
    load, send1, recv1, send2, recv2, send3, recv3,
    isend1, irecv1, isend2, irecv2, isend3, irecv3,
    dsend1, drecv1, dsend2, drecv2,
):
    nb = na
    nk = 2 * nb // nx
    nj = nb // nx
    half = nx // 2
    rows, feat = emb_ref.shape
    hf = feat // 2
    chunk = nb * nx * CAP
    wide = nx * CAP
    per_step = nx * nk * CAP
    lanes = 128
    group = 4

    loads = [
        pltpu.make_async_copy(src, dst, load.at[i])
        for i, (src, dst) in enumerate(
            [(home_hbm, home_ref), (cluster_hbm, cluster_ref), (emb_hbm, emb_ref)]
        )
    ]
    for copy in loads:
        copy.start()

    shard = lax.axis_index("shard")
    x = lax.axis_index("tile")
    core = lax.rem(shard, 2)
    y = lax.rem(lax.div(shard, 2), nb)
    z = lax.div(shard, 2 * nb)
    a = z + core * (y - z)
    b = y + core * (z - y)

    def on(a_to, b_to):
        z_to = a_to + core * (b_to - a_to)
        y_to = b_to + core * (a_to - b_to)
        return (z_to * nb + y_to) * 2 + core

    sibling = (shard + 1 - 2 * core, x)

    def delta(t):
        return ((t + 1) // 2 * (2 * (t % 2) - 1)) % na

    ahead = [on(lax.rem(a + delta(t), na), b) for t in range(na)]
    behind = [on(lax.rem(a + na - delta(t), na), b) for t in range(na)]
    ring = [on(a, i) for i in range(nb)]
    b_to = [lax.rem(x - a - half * (k // nj) + nx + na * nx, nx) + nx * (k % nj) for k in range(nk)]
    owner = [on(a, b_to[k]) for k in range(nk)]
    stays = [b_to[k] == b for k in range(nk)]
    turn = lax.rem(x - a - b + 2 * na * nx, nx)
    computes = lax.rem(turn, half) == 0
    k_self = lax.div(turn, half) * nj + lax.div(b, nx)

    def either(same, local, remote):
        pl.when(same)(local)
        pl.when(jnp.logical_not(same))(remote)

    barrier = pltpu.get_barrier_semaphore()

    def greet(device):
        pl.semaphore_signal(barrier, inc=1, device_id=device, device_id_type=MESH)

    for t in range(na):
        for xs in range(nx):
            if t == 0:
                @pl.when(x != xs)
                def _():
                    greet((ahead[t], xs))
            else:
                greet((ahead[t], xs))
    for i in range(nb):
        @pl.when(b != i)
        def _():
            greet((ring[i], x))
    greet(sibling)

    loads[0].wait()
    home = home_ref[...]
    named = iota((2 * na * nb, rows), 0) == home
    before = (iota((rows, rows), 0) < iota((rows, rows), 1)).astype(BF16)
    counts = jnp.dot(named.astype(BF16), before, preferred_element_type=F32)
    pos = jnp.sum(jnp.where(named, counts, 0.0), axis=0, keepdims=True).astype(I32)
    c_own = home % 2
    y_own = (home // 2) % nb
    z_own = home // (2 * nb)
    a_own = z_own + core * (y_own - z_own)
    b_own = y_own + core * (z_own - y_own)
    x_own = (a_own + b_own + half * c_own) % nx
    k_own = c_own * nj + b_own // nx
    step = (a_own - a + na) % na
    step = jnp.where(step <= na // 2, jnp.maximum(2 * step - 1, 0), 2 * (na - step))
    message = step * nx + x_own
    lane = k_own * CAP + pos
    slot = message * (nk * CAP) + lane

    loads[2].wait()
    values = emb_ref[...].astype(F32)
    unit[...] = (
        values * lax.rsqrt(jnp.sum(values * values, axis=1, keepdims=True) + 1e-06)
    ).astype(BF16)

    loads[1].wait()
    marks = (cluster_ref[...] + 1).astype(F32)
    in_message = (iota((na * nx, rows), 0) == message).astype(BF16)
    in_lane = jnp.where(iota((lanes, rows), 0) == lane, marks, 0.0).astype(BF16)
    tags = nt_dot(in_message, in_lane)
    for m in range(na * nx):
        ids1[m] = tags[m : m + 1]

    pl.semaphore_wait(barrier, na * nx - 1 + nb - 1 + 1)

    def ids1_copy(t, xs):
        return pltpu.make_async_remote_copy(
            src_ref=ids1.at[t * nx + xs], dst_ref=ids1_in.at[t * nx + x],
            send_sem=isend1.at[t, xs], recv_sem=irecv1,
            device_id=(ahead[t], xs), device_id_type=MESH,
        )

    def out1_copy(t, xs):
        return pltpu.make_async_remote_copy(
            src_ref=out1.at[t, xs], dst_ref=in1.at[t, x],
            send_sem=send1.at[t, xs], recv_sem=recv1.at[t],
            device_id=(ahead[t], xs), device_id_type=MESH,
        )

    def place(t):
        pick = (iota((per_step, rows), 0) + t * per_step == slot).astype(BF16)
        placed = jnp.dot(pick, unit[...], preferred_element_type=F32)
        placed = placed.reshape(nx * nk, CAP, feat)
        placed = jnp.concatenate([placed[:, :, :hf], placed[:, :, hf:]], axis=1).astype(BF16)
        out1[t] = placed.reshape(nx, nk, 2 * CAP, hf)
        for xs in range(nx):
            if t > 0:
                out1_copy(t, xs).start()
            else:
                either(
                    x == xs,
                    lambda: pltpu.make_async_copy(out1.at[0, x], in1.at[0, x], recv1.at[0]).start(),
                    lambda: out1_copy(t, xs).start(),
                )

    def ids1_send():
        for t in range(na):
            for xs in range(nx):
                if t > 0:
                    ids1_copy(t, xs).start()
                else:
                    either(
                        x == xs,
                        lambda: pltpu.make_async_copy(ids1.at[x], ids1_in.at[x], irecv1).start(),
                        lambda: ids1_copy(t, xs).start(),
                    )

    for t in range(na):
        if t == min(3, na - 1):
            ids1_send()
        place(t)

    at_lane = iota((na, lanes), 1)

    def shifted(block, source, target):
        mine = jnp.where((at_lane >= source * CAP) & (at_lane < source * CAP + CAP), block, 0.0)
        turns = ((target - source) * CAP) % lanes
        return pltpu.roll(mine, turns, 1) if turns else mine

    def ids2_copy(k):
        return pltpu.make_async_remote_copy(
            src_ref=ids2.at[k], dst_ref=ids2_in.at[b],
            send_sem=isend2.at[k], recv_sem=irecv2,
            device_id=(owner[k], x), device_id_type=MESH,
        )

    def rows2_copy(t, k):
        return pltpu.make_async_remote_copy(
            src_ref=in1.at[t, :, k], dst_ref=in2.at[t, b],
            send_sem=send2.at[t, k], recv_sem=recv2.at[t],
            device_id=(owner[k], x), device_id_type=MESH,
        )

    def forward_ids():
        pltpu.make_async_copy(ids1, ids1_in, irecv1).wait()
        tags_in = [
            jnp.concatenate([ids1_in[t * nx + xs] for t in range(na)], axis=0)
            for xs in range(nx)
        ]
        for k in range(nk):
            ids2[k] = functools.reduce(jnp.add, [shifted(tags_in[xs], k, xs) for xs in range(nx)])
            either(
                stays[k],
                lambda: pltpu.make_async_copy(ids2.at[k], ids2_in.at[b], irecv2).start(),
                lambda: ids2_copy(k).start(),
            )

    for t in range(na):
        pltpu.make_async_copy(in1.at[t], in1.at[t], recv1.at[t]).wait()
        for k in range(nk):
            either(
                stays[k],
                lambda: pltpu.make_async_copy(
                    in1.at[t, :, k], in2.at[t, b], recv2.at[t]
                ).start(),
                lambda: rows2_copy(t, k).start(),
            )
        if t == min(2, na - 1):
            forward_ids()

    for t in range(na):
        for xs in range(nx):
            def sent(t=t, xs=xs):
                ids1_copy(t, xs).wait_send()
                out1_copy(t, xs).wait_send()

            if t > 0:
                sent()
            else:
                pl.when(x != xs)(sent)

    def sib_ids_copy():
        return pltpu.make_async_remote_copy(
            src_ref=ids2_in, dst_ref=ids2_sib, send_sem=isend3, recv_sem=irecv3,
            device_id=sibling, device_id_type=MESH,
        )

    def sib_rows_copy(t):
        return pltpu.make_async_remote_copy(
            src_ref=kept.at[0, t], dst_ref=sib_in.at[t],
            send_sem=send3.at[t], recv_sem=recv3.at[t],
            device_id=sibling, device_id_type=MESH,
        )

    def spread_ids(source, side):
        same = iota((chunk, lanes), 1) == iota((chunk, lanes), 0) % wide

        def spread(t, carry):
            block = jnp.concatenate(
                [
                    jnp.broadcast_to(source[j, pl.ds(t, 1), :], (wide, lanes))
                    for j in range(nb)
                ],
                axis=0,
            )
            block = jnp.where(same, block, 0.0)
            row_ids[side, t] = jnp.broadcast_to(
                jnp.sum(block, axis=1, keepdims=True), (chunk, lanes)
            )
            key_ids[side, t] = nt_dot(jnp.ones((8, lanes), BF16), block.astype(BF16))
            return carry

        lax.fori_loop(0, na, spread, 0)

    def tile(side, g, key_side, t, last, by_row, by_col, sums):
        left = kept[side, pl.ds(g * group, group)].reshape(group * chunk, feat)
        scores = nt_dot(left, kept[key_side, t])
        weights = jnp.exp2(scores * SCALE)
        theirs = key_ids[key_side, t, 0:1, :]
        for i in range(group):
            at = g * group + i
            mine = row_ids[side, at]
            valid = jnp.where(at <= last, theirs, -1.0)
            matched = [
                jnp.where(
                    mine == valid[:, j : j + lanes],
                    weights[i * chunk : (i + 1) * chunk, j : j + lanes],
                    0.0,
                )
                for j in range(0, chunk, lanes)
            ]
            if by_row:
                acc[at] += functools.reduce(jnp.add, matched)
            if by_col:
                parts = [jnp.sum(m.reshape(chunk // 8, 8, lanes), axis=0) for m in matched]
                part = jnp.concatenate(parts, axis=1)
                if by_row:
                    part = jnp.where(at < t, part, 0.0)
                sums += part
        return sums

    def pair_sums(t, carry):
        pltpu.make_async_copy(in2.at[t], in2.at[t], recv2.at[t]).wait()
        block = in2[t].reshape(nb * nx, 2 * CAP, hf).astype(F32)
        block = jnp.concatenate([block[:, :CAP, :], block[:, CAP:, :]], axis=2)
        kept[0, t] = block.reshape(chunk, feat).astype(BF16)
        sib_rows_copy(t).start()
        groups = lax.div(t + group, group)
        sums = lax.fori_loop(
            0, groups, lambda g, c: tile(0, g, 0, t, t, True, True, c),
            jnp.zeros((8, chunk), F32),
        )

        @pl.when(t == 0)
        def _():
            sib_ids_copy().wait_recv()
            spread_ids(ids2_sib, 1)

        sib_rows_copy(t).wait_recv()
        kept[1, t] = sib_in[t]
        sums = lax.fori_loop(
            0, groups, lambda g, c: tile(1, g, 0, t, t, False, True, c), sums
        )
        col[pl.ds(t, 1), :] = jnp.sum(sums, axis=0, keepdims=True)
        lax.fori_loop(
            0, lax.div(t + group - 1, group),
            lambda g, c: tile(0, g, 1, t, t - 1, True, False, c), 0,
        )
        return carry

    def den1_copy(to):
        return pltpu.make_async_remote_copy(
            src_ref=den.at[to], dst_ref=den_in.at[k_self],
            send_sem=dsend1.at[to], recv_sem=drecv1,
            device_id=(ring[to], x), device_id_type=MESH,
        )

    @pl.when(computes)
    def _():
        pltpu.make_async_copy(ids2_in, ids2_in, irecv2).wait()
        sib_ids_copy().start()
        spread_ids(ids2_in, 0)
        acc[...] = jnp.zeros_like(acc)
        lax.fori_loop(0, na, pair_sums, 0)

        same = iota((chunk, lanes), 1) == iota((chunk, lanes), 0) % wide
        for t in range(na):
            sums = jnp.sum(acc[t], axis=1, keepdims=True)
            block = jnp.where(same, sums, 0.0).reshape(nb, wide, lanes)
            block = jnp.sum(block, axis=1)
            for j in range(nb):
                den[j, t : t + 1, :] = block[j : j + 1]
        by_col = col[...]
        per = lanes // wide
        for j in range(nb):
            part = by_col[:, j // per * lanes : (j // per + 1) * lanes]
            turns = (-(j % per) * wide) % lanes
            part = pltpu.roll(part, turns, 1) if turns else part
            part = jnp.where(at_lane < wide, part, 0.0)
            den[j] = (den[j] + part) * (2.0 ** (-SCALE))
            either(
                b == j,
                lambda: pltpu.make_async_copy(den.at[j], den_in.at[k_self], drecv1).start(),
                lambda: den1_copy(j).start(),
            )

    for k in range(nk):
        @pl.when(jnp.logical_not(stays[k]))
        def _():
            ids2_copy(k).wait_send()
            for t in range(na):
                rows2_copy(t, k).wait_send()

    pltpu.make_async_copy(den_in, den_in, drecv1).wait()

    def ret_copy(t, xs):
        return pltpu.make_async_remote_copy(
            src_ref=ret.at[t * nx + xs], dst_ref=ret_in.at[t * nx + x],
            send_sem=dsend2.at[t, xs], recv_sem=drecv2,
            device_id=(behind[t], xs), device_id_type=MESH,
        )

    for xs in range(nx):
        block = functools.reduce(jnp.add, [shifted(den_in[k], xs, k) for k in range(nk)])
        for t in range(na):
            ret[t * nx + xs] = block[t : t + 1]
            if t > 0:
                ret_copy(t, xs).start()
            else:
                either(
                    x == xs,
                    lambda: pltpu.make_async_copy(ret.at[x], ret_in.at[x], drecv2).start(),
                    lambda: ret_copy(t, xs).start(),
                )

    @pl.when(computes)
    def _():
        sib_ids_copy().wait_send()
        for t in range(na):
            sib_rows_copy(t).wait_send()

            @pl.when(b != t)
            def _():
                den1_copy(t).wait_send()

    chosen = (iota((lanes, rows), 0) == message).astype(BF16)
    pltpu.make_async_copy(ret, ret_in, drecv2).wait()

    table = jnp.concatenate(
        [ret_in[m] for m in range(na * nx)] + [jnp.zeros((lanes - na * nx, lanes), F32)], axis=0
    )
    table = table.T[: nk * CAP]
    high = table.astype(BF16)
    rest = table - high.astype(F32)
    mid = rest.astype(BF16)
    low = (rest - mid.astype(F32)).astype(BF16)
    picked = (
        jnp.dot(low, chosen, preferred_element_type=F32)
        + jnp.dot(mid, chosen, preferred_element_type=F32)
    ) + jnp.dot(high, chosen, preferred_element_type=F32)
    out_ref[...] = jnp.sum(
        jnp.where(iota((nk * CAP, rows), 0) == lane, picked, 0.0), axis=0, keepdims=True
    )

    for t in range(na):
        for xs in range(nx):
            if t > 0:
                ret_copy(t, xs).wait_send()
            else:
                @pl.when(x != xs)
                def _():
                    ret_copy(t, xs).wait_send()


def shards(n_tile, embeddings, cluster, home):
    n_shard = lax.axis_size("shard")
    na = next(n for n in range(1, n_shard + 1) if 2 * n * n == n_shard)
    nx = n_tile
    nk = 2 * na // nx
    rows, feat = embeddings.shape
    chunk = na * nx * CAP
    hf = feat // 2
    messages = na * nx
    vmem = pltpu.VMEM
    dma = pltpu.SemaphoreType.DMA
    out = pl.pallas_call(
        functools.partial(kernel, na, nx),
        out_shape=jax.ShapeDtypeStruct((1, rows), F32),
        in_specs=[pl.BlockSpec(memory_space=pl.ANY)] * 3,
        out_specs=pl.BlockSpec(memory_space=pltpu.VMEM),
        scratch_shapes=[
            vmem((1, rows), I32),
            vmem((1, rows), I32),
            vmem((rows, feat), BF16),
            vmem((rows, feat), BF16),
            vmem((na, nx, nk, 2 * CAP, hf), BF16),
            vmem((na, nx, nk, 2 * CAP, hf), BF16),
            vmem((na, na, nx, 2 * CAP, hf), BF16),
            vmem((na, chunk, feat), BF16),
            vmem((2, na, chunk, feat), BF16),
            vmem((na, chunk, 128), F32),
            vmem((na, chunk), F32),
            vmem((messages, 1, 128), F32),
            vmem((messages, 1, 128), F32),
            vmem((nk, na, 128), F32),
            vmem((na, na, 128), F32),
            vmem((na, na, 128), F32),
            vmem((2, na, 8, chunk), F32),
            vmem((2, na, chunk, 128), F32),
            vmem((na, na, 128), F32),
            vmem((nk, na, 128), F32),
            vmem((messages, 1, 128), F32),
            vmem((messages, 1, 128), F32),
            dma((3,)),
            dma((na, nx)), dma((na,)), dma((na, nk)), dma((na,)), dma((na,)), dma((na,)),
            dma((na, nx)), dma(()), dma((nk,)), dma(()), dma(()), dma(()),
            dma((na,)), dma(()), dma((na, nx)), dma(()),
        ],
        compiler_params=pltpu.CompilerParams(
            collective_id=0, has_side_effects=True, vmem_limit_bytes=48 * 2**20
        ),
    )(home.reshape(1, rows), cluster.reshape(1, rows), embeddings)
    return out.reshape(rows)


def solution(mesh):
    return jax.shard_map(
        functools.partial(shards, mesh.shape["tile"]),
        mesh=mesh,
        in_specs=(P(("shard", "tile"), None), P(("shard", "tile")), P(("shard", "tile"))),
        out_specs=P(("shard", "tile")),
        check_vma=False,
    )
```

```python
import functools

import jax
import jax.numpy as jnp
from jax import lax
from jax.experimental import pallas as pl
from jax.experimental.pallas import tpu as pltpu
from jax.sharding import PartitionSpec as P

F32 = jnp.float32
BF16 = jnp.bfloat16
I32 = jnp.int32
MESH = pl.DeviceIdType.MESH
CAP = 8
SCALE = 10.0 * 1.4426950408889634


def iota(shape, dim):
    return lax.broadcasted_iota(I32, shape, dim)


def nt_dot(left, right):
    return lax.dot_general(left, right, (((1,), (1,)), ((), ())), preferred_element_type=F32)


def kernel(
    na, nx, home_hbm, cluster_hbm, emb_hbm, out_ref,
    home_ref, cluster_ref, emb_ref, unit, out1, in1, in2, sib_in, kept, acc, col,
    ids1, ids1_in, ids2, ids2_in, ids3_in, ids_sib, key_ids, row_ids,
    den, den_in, ret, ret_in,
    load, send1, recv1, send2, recv2, send3, recv3,
    isend1, irecv1, isend2, irecv2, isend3, irecv3, isend4, irecv4,
    dsend1, drecv1, dsend2, drecv2,
):
    nb = na
    nk = 2 * nb // nx
    nj = nb // nx
    half = nx // 2
    rows, feat = emb_ref.shape
    hf = feat // 2
    ns = na // 2
    nq = 2 * nx
    chunk = nb * ns * CAP
    wide = ns * CAP
    lanes = 128
    group = 4

    loads = [
        pltpu.make_async_copy(src, dst, load.at[i])
        for i, (src, dst) in enumerate(
            [(home_hbm, home_ref), (cluster_hbm, cluster_ref), (emb_hbm, emb_ref)]
        )
    ]
    for copy in loads:
        copy.start()

    shard = lax.axis_index("shard")
    x = lax.axis_index("tile")
    core = lax.rem(shard, 2)
    y = lax.rem(lax.div(shard, 2), nb)
    z = lax.div(shard, 2 * nb)
    a = z + core * (y - z)
    b = y + core * (z - y)

    def on(a_to, b_to):
        z_to = a_to + core * (b_to - a_to)
        y_to = b_to + core * (a_to - b_to)
        return (z_to * nb + y_to) * 2 + core

    sibling = (shard + 1 - 2 * core, x)

    def delta(t):
        return ((t + 1) // 2 * (2 * (t % 2) - 1)) % na

    ahead = [on(lax.rem(a + delta(t), na), b) for t in range(na)]
    behind = [on(lax.rem(a + na - delta(t), na), b) for t in range(na)]
    ring = [on(a, i) for i in range(nb)]
    b_to = [lax.rem(x - a - half * (k // nj) + nx + na * nx, nx) + nx * (k % nj) for k in range(nk)]
    owner = [on(a, b_to[k]) for k in range(nk)]
    stays = [b_to[k] == b for k in range(nk)]
    turn = lax.rem(x - a - b + 2 * na * nx, nx)
    computes = lax.rem(turn, half) == 0
    k_self = lax.div(turn, half) * nj + lax.div(b, nx)
    k_sib = lax.div(turn, half) * nj + lax.div(a, nx)

    def either(same, local, remote):
        pl.when(same)(local)
        pl.when(jnp.logical_not(same))(remote)

    def right(j):
        return lax.rem(x + j, nx)

    def left(j):
        return lax.rem(x + nx - j, nx)

    barrier = pltpu.get_barrier_semaphore()

    def greet(device):
        pl.semaphore_signal(barrier, inc=1, device_id=device, device_id_type=MESH)

    for j in range(nx):
        for t in range(na):
            if j + t > 0:
                greet((ahead[t], right(j)))
    for i in range(nb):
        @pl.when(b != i)
        def _():
            greet((ring[i], x))
    greet(sibling)

    loads[0].wait()
    home = home_ref[...]
    named = iota((2 * na * nb, rows), 0) == home
    before = (iota((rows, rows), 0) < iota((rows, rows), 1)).astype(BF16)
    counts = jnp.dot(named.astype(BF16), before, preferred_element_type=F32)
    pos = jnp.sum(jnp.where(named, counts, 0.0), axis=0, keepdims=True).astype(I32)
    c_own = home % 2
    y_own = (home // 2) % nb
    z_own = home // (2 * nb)
    a_own = z_own + core * (y_own - z_own)
    b_own = y_own + core * (z_own - y_own)
    x_own = (a_own + b_own + half * c_own) % nx
    k_own = c_own * nj + b_own // nx
    step = (a_own - a + na) % na
    step = jnp.where(step <= na // 2, jnp.maximum(2 * step - 1, 0), 2 * (na - step))
    offset = (x_own - x + nx) % nx
    message = offset * na + step
    lane = k_own * CAP + pos
    slot = message * (nk * CAP) + lane

    loads[2].wait()
    values = emb_ref[...].astype(F32)
    unit[...] = (
        values * lax.rsqrt(jnp.sum(values * values, axis=1, keepdims=True) + 1e-06)
    ).astype(BF16)

    loads[1].wait()
    marks = (cluster_ref[...] + 1).astype(F32)
    in_step = (iota((na, rows), 0) == step).astype(BF16)
    in_lane = jnp.where(iota((lanes, rows), 0) == offset * (nk * CAP) + lane, marks, 0.0)
    tags = nt_dot(in_step, in_lane.astype(BF16))
    for t in range(na):
        ids1[t] = tags[t : t + 1]

    pl.semaphore_wait(barrier, na * nx - 1 + nb - 1 + 1)

    def ids1_copy(t):
        return pltpu.make_async_remote_copy(
            src_ref=ids1.at[t], dst_ref=ids1_in.at[t],
            send_sem=isend1.at[t], recv_sem=irecv1,
            device_id=(ahead[t], x), device_id_type=MESH,
        )

    def ids2_copy(i):
        return pltpu.make_async_remote_copy(
            src_ref=ids2, dst_ref=ids2_in.at[b],
            send_sem=isend2.at[i], recv_sem=irecv2,
            device_id=(ring[i], x), device_id_type=MESH,
        )

    def ids3_copy(j):
        return pltpu.make_async_remote_copy(
            src_ref=ids2_in, dst_ref=ids3_in.at[j],
            send_sem=isend3.at[j], recv_sem=irecv3,
            device_id=(shard, right(j)), device_id_type=MESH,
        )

    def out1_copy(j, t):
        q, sub = j * 2 + t // ns, t % ns
        return pltpu.make_async_remote_copy(
            src_ref=out1.at[q, sub], dst_ref=in1.at[q, sub],
            send_sem=send1.at[j, t], recv_sem=recv1.at[j],
            device_id=(ahead[t], right(j)), device_id_type=MESH,
        )

    def place(j, h):
        q = j * 2 + h
        size = ns * nk * CAP
        pick = (iota((size, rows), 0) + q * size == slot).astype(BF16)
        placed = jnp.dot(pick, unit[...], preferred_element_type=F32)
        placed = placed.reshape(ns * nk, CAP, feat)
        placed = jnp.concatenate([placed[:, :, :hf], placed[:, :, hf:]], axis=1).astype(BF16)
        out1[q] = placed.reshape(ns, nk, 2 * CAP, hf)

    def send_stage(j, first):
        for h in range(2):
            place(j, h)
            for t in range(h * ns, (h + 1) * ns):
                if first and t == 0:
                    pltpu.make_async_copy(out1.at[0, 0], in1.at[0, 0], recv1.at[0]).start()
                else:
                    out1_copy(j, t).start()

    def sent_stage(j):
        for t in range(na):
            if t > 0:
                out1_copy(j, t).wait_send()
            else:
                @pl.when(j > 0)
                def _():
                    out1_copy(j, t).wait_send()

    def rows2_copy(q, k):
        return pltpu.make_async_remote_copy(
            src_ref=in1.at[q, :, k], dst_ref=in2.at[q, b],
            send_sem=send2.at[q, k], recv_sem=recv2.at[q],
            device_id=(owner[k], x), device_id_type=MESH,
        )

    def forward_stage(j):
        for h in range(2):
            q = j * 2 + h
            for k in range(nk):
                either(
                    stays[k],
                    lambda: pltpu.make_async_copy(
                        in1.at[q, :, k], in2.at[q, b], recv2.at[q]
                    ).start(),
                    lambda: rows2_copy(q, k).start(),
                )

    def forwarded_stage(j):
        for k in range(nk):
            @pl.when(jnp.logical_not(stays[k]))
            def _():
                for h in range(2):
                    rows2_copy(j * 2 + h, k).wait_send()

    def sib_ids_copy():
        return pltpu.make_async_remote_copy(
            src_ref=ids3_in, dst_ref=ids_sib, send_sem=isend4, recv_sem=irecv4,
            device_id=sibling, device_id_type=MESH,
        )

    def sib_rows_copy(t):
        return pltpu.make_async_remote_copy(
            src_ref=kept.at[0, t], dst_ref=sib_in.at[t],
            send_sem=send3.at[t], recv_sem=recv3.at[t],
            device_id=sibling, device_id_type=MESH,
        )

    def spread_ids(source, side, k):
        def spread(q, carry):
            j, h = lax.div(q, 2), lax.rem(q, 2)
            block = jnp.concatenate(
                [source[j, i, pl.ds(h * ns, ns), :] for i in range(nb)], axis=0
            )
            block = jnp.broadcast_to(block[:, None, :], (nb * ns, CAP, lanes))
            here = iota((nb * ns, CAP, lanes), 1) + (j * nk + k) * CAP
            block = jnp.where(iota((nb * ns, CAP, lanes), 2) == here, block, 0.0)
            block = block.reshape(chunk, lanes)
            row_ids[side, q] = jnp.broadcast_to(
                jnp.sum(block, axis=1, keepdims=True), (chunk, lanes)
            )
            key_ids[side, q] = nt_dot(jnp.ones((8, lanes), BF16), block.astype(BF16))
            return carry

        lax.fori_loop(0, nq, spread, 0)

    def tile(side, g, key_side, t, last, by_row, by_col, sums):
        left = kept[side, pl.ds(g * group, group)].reshape(group * chunk, feat)
        scores = nt_dot(left, kept[key_side, t])
        weights = jnp.exp2(scores * SCALE)
        theirs = key_ids[key_side, t, 0:1, :]
        for i in range(group):
            at = g * group + i
            mine = row_ids[side, at]
            valid = jnp.where(at <= last, theirs, -1.0)
            matched = [
                jnp.where(
                    mine == valid[:, j : j + lanes],
                    weights[i * chunk : (i + 1) * chunk, j : j + lanes],
                    0.0,
                )
                for j in range(0, chunk, lanes)
            ]
            if by_row:
                acc[at] += functools.reduce(jnp.add, matched)
            if by_col:
                parts = [jnp.sum(m.reshape(chunk // 8, 8, lanes), axis=0) for m in matched]
                part = jnp.concatenate(parts, axis=1)
                if by_row:
                    part = jnp.where(at < t, part, 0.0)
                sums += part
        return sums

    def take(t, carry):
        pltpu.make_async_copy(in2.at[t], in2.at[t], recv2.at[t]).wait()
        block = in2[t].reshape(nb * ns, 2 * CAP, hf).astype(F32)
        block = jnp.concatenate([block[:, :CAP, :], block[:, CAP:, :]], axis=2)
        kept[0, t] = block.reshape(chunk, feat).astype(BF16)
        sib_rows_copy(t).start()
        return carry

    def pair_sums(t, carry):
        groups = lax.div(t + group, group)
        sums = lax.fori_loop(
            0, groups, lambda g, c: tile(0, g, 0, t, t, True, True, c),
            jnp.zeros((8, chunk), F32),
        )
        sib_rows_copy(t).wait_recv()
        kept[1, t] = sib_in[t]
        sums = lax.fori_loop(
            0, groups, lambda g, c: tile(1, g, 0, t, t, False, True, c), sums
        )
        col[pl.ds(t, 1), :] = jnp.sum(sums, axis=0, keepdims=True)
        lax.fori_loop(
            0, lax.div(t + group - 1, group),
            lambda g, c: tile(0, g, 1, t, t - 1, True, False, c), 0,
        )
        return carry

    pltpu.make_async_copy(ids1.at[0], ids1_in.at[0], irecv1).start()
    for t in range(1, na):
        ids1_copy(t).start()
    send_stage(0, True)
    pltpu.make_async_copy(ids1, ids1_in, irecv1).wait()
    ids2[...] = jnp.concatenate([ids1_in[t] for t in range(na)], axis=0)
    for i in range(nb):
        either(
            b == i,
            lambda: pltpu.make_async_copy(ids2, ids2_in.at[b], irecv2).start(),
            lambda: ids2_copy(i).start(),
        )
    send_stage(1, False)
    pltpu.make_async_copy(ids2_in, ids2_in, irecv2).wait()
    pltpu.make_async_copy(ids2_in, ids3_in.at[0], irecv3).start()
    for j in range(1, nx):
        ids3_copy(j).start()

    def stage(j, carry):
        @pl.when(j < nx)
        def _():
            here = in1.at[pl.ds(2 * j, 2)]
            pltpu.make_async_copy(here, here, recv1.at[j]).wait()

            @pl.when(j >= 2)
            def _():
                forwarded_stage(j - 2)

            forward_stage(j)

            @pl.when(j < nx - 2)
            def _():
                sent_stage(j)
                send_stage(j + 2, False)

        @pl.when(computes & (j == 0))
        def _():
            pltpu.make_async_copy(ids3_in, ids3_in, irecv3).wait()
            sib_ids_copy().start()
            spread_ids(ids3_in, 0, k_self)
            acc[...] = jnp.zeros_like(acc)

        @pl.when(computes & (j == 1))
        def _():
            sib_ids_copy().wait_recv()
            spread_ids(ids_sib, 1, k_sib)

        @pl.when(computes & (j > 0))
        def _():
            lax.fori_loop(2 * j - 2, 2 * j, take, 0)
            lax.fori_loop(2 * j - 2, 2 * j, pair_sums, 0)
        return carry

    lax.fori_loop(0, nx + 1, stage, 0)

    def den1_copy(to):
        return pltpu.make_async_remote_copy(
            src_ref=den.at[to], dst_ref=den_in.at[k_self],
            send_sem=dsend1.at[to], recv_sem=drecv1,
            device_id=(ring[to], x), device_id_type=MESH,
        )

    @pl.when(computes)
    def _():
        same = iota((chunk, lanes), 1) == iota((chunk, lanes), 0) % wide
        for t in range(nq):
            sums = jnp.sum(acc[t], axis=1, keepdims=True)
            block = jnp.where(same, sums, 0.0).reshape(nb, wide, lanes)
            block = jnp.sum(block, axis=1)
            for j in range(nb):
                den[j, t : t + 1, :] = block[j : j + 1]
        by_col = col[...]
        per = lanes // wide
        for j in range(nb):
            part = by_col[:, j // per * lanes : (j // per + 1) * lanes]
            turns = (-(j % per) * wide) % lanes
            part = pltpu.roll(part, turns, 1) if turns else part
            part = jnp.where(iota((nq, lanes), 1) < wide, part, 0.0)
            den[j] = (den[j] + part) * (2.0 ** (-SCALE))
            either(
                b == j,
                lambda: pltpu.make_async_copy(den.at[j], den_in.at[k_self], drecv1).start(),
                lambda: den1_copy(j).start(),
            )

    @pl.when(jnp.logical_not(computes))
    def _():
        pltpu.make_async_copy(ids3_in, ids3_in, irecv3).wait()

    for j in range(nx - 2, nx):
        sent_stage(j)
        forwarded_stage(j)
    for i in range(1, na):
        ids1_copy(i).wait_send()
    for i in range(nb):
        @pl.when(b != i)
        def _():
            ids2_copy(i).wait_send()
    for j in range(1, nx):
        ids3_copy(j).wait_send()

    at_lane = iota((nq, lanes), 1)

    def shifted(block, source, target):
        mine = jnp.where((at_lane >= source * CAP) & (at_lane < source * CAP + CAP), block, 0.0)
        turns = ((target - source) * CAP) % lanes
        return pltpu.roll(mine, turns, 1) if turns else mine

    pltpu.make_async_copy(den_in, den_in, drecv1).wait()

    def ret_copy(q, sub):
        return pltpu.make_async_remote_copy(
            src_ref=ret.at[q * ns + sub], dst_ref=ret_in.at[q * ns + sub],
            send_sem=dsend2.at[q, sub], recv_sem=drecv2,
            device_id=(behind[q % 2 * ns + sub], left(q // 2)), device_id_type=MESH,
        )

    for sub in range(ns):
        block = functools.reduce(jnp.add, [shifted(den_in[k], sub, k) for k in range(nk)])
        for q in range(nq):
            ret[q * ns + sub] = block[q : q + 1]
            if q + sub > 0:
                ret_copy(q, sub).start()
            else:
                pltpu.make_async_copy(ret.at[0], ret_in.at[0], drecv2).start()

    @pl.when(computes)
    def _():
        sib_ids_copy().wait_send()
        for q in range(nq):
            sib_rows_copy(q).wait_send()
        for i in range(nb):
            @pl.when(b != i)
            def _():
                den1_copy(i).wait_send()

    chosen = (iota((lanes, rows), 0) == message).astype(BF16)
    pltpu.make_async_copy(ret, ret_in, drecv2).wait()

    table = jnp.concatenate(
        [ret_in[m] for m in range(na * nx)] + [jnp.zeros((lanes - na * nx, lanes), F32)], axis=0
    )
    table = table.T[: nk * CAP]
    high = table.astype(BF16)
    rest = table - high.astype(F32)
    mid = rest.astype(BF16)
    low = (rest - mid.astype(F32)).astype(BF16)
    picked = (
        jnp.dot(low, chosen, preferred_element_type=F32)
        + jnp.dot(mid, chosen, preferred_element_type=F32)
    ) + jnp.dot(high, chosen, preferred_element_type=F32)
    out_ref[...] = jnp.sum(
        jnp.where(iota((nk * CAP, rows), 0) == lane, picked, 0.0), axis=0, keepdims=True
    )

    for q in range(nq):
        for sub in range(ns):
            if q + sub > 0:
                ret_copy(q, sub).wait_send()


def shards(n_tile, embeddings, cluster, home):
    n_shard = lax.axis_size("shard")
    na = next(n for n in range(1, n_shard + 1) if 2 * n * n == n_shard)
    nx = n_tile
    nk = 2 * na // nx
    rows, feat = embeddings.shape
    ns = na // 2
    nq = 2 * nx
    chunk = na * ns * CAP
    hf = feat // 2
    messages = na * nx
    vmem = pltpu.VMEM
    dma = pltpu.SemaphoreType.DMA
    out = pl.pallas_call(
        functools.partial(kernel, na, nx),
        out_shape=jax.ShapeDtypeStruct((1, rows), F32),
        in_specs=[pl.BlockSpec(memory_space=pl.ANY)] * 3,
        out_specs=pl.BlockSpec(memory_space=pltpu.VMEM),
        scratch_shapes=[
            vmem((1, rows), I32),
            vmem((1, rows), I32),
            vmem((rows, feat), BF16),
            vmem((rows, feat), BF16),
            vmem((nq, ns, nk, 2 * CAP, hf), BF16),
            vmem((nq, ns, nk, 2 * CAP, hf), BF16),
            vmem((nq, na, ns, 2 * CAP, hf), BF16),
            vmem((nq, chunk, feat), BF16),
            vmem((2, nq, chunk, feat), BF16),
            vmem((nq, chunk, 128), F32),
            vmem((nq, chunk), F32),
            vmem((na, 1, 128), F32),
            vmem((na, 1, 128), F32),
            vmem((na, 128), F32),
            vmem((na, na, 128), F32),
            vmem((nx, na, na, 128), F32),
            vmem((nx, na, na, 128), F32),
            vmem((2, nq, 8, chunk), F32),
            vmem((2, nq, chunk, 128), F32),
            vmem((na, nq, 128), F32),
            vmem((nk, nq, 128), F32),
            vmem((messages, 1, 128), F32),
            vmem((messages, 1, 128), F32),
            dma((3,)),
            dma((nx, na)), dma((nx,)), dma((nq, nk)), dma((nq,)), dma((nq,)), dma((nq,)),
            dma((na,)), dma(()), dma((na,)), dma(()), dma((nx,)), dma(()), dma(()), dma(()),
            dma((na,)), dma(()), dma((nq, ns)), dma(()),
        ],
        compiler_params=pltpu.CompilerParams(
            collective_id=0, has_side_effects=True, vmem_limit_bytes=48 * 2**20
        ),
    )(home.reshape(1, rows), cluster.reshape(1, rows), embeddings)
    return out.reshape(rows)


def solution(mesh):
    return jax.shard_map(
        functools.partial(shards, mesh.shape["tile"]),
        mesh=mesh,
        in_specs=(P(("shard", "tile"), None), P(("shard", "tile")), P(("shard", "tile"))),
        out_specs=P(("shard", "tile")),
        check_vma=False,
    )
```

```python
import functools

import jax
import jax.numpy as jnp
from jax import lax
from jax.experimental import pallas as pl
from jax.experimental.pallas import tpu as pltpu
from jax.sharding import PartitionSpec as P

F32 = jnp.float32
BF16 = jnp.bfloat16
I32 = jnp.int32
MESH = pl.DeviceIdType.MESH
CAP = 8
SCALE = 10.0 * 1.4426950408889634


def iota(shape, dim):
    return lax.broadcasted_iota(I32, shape, dim)


def nt_dot(left, right):
    return lax.dot_general(left, right, (((1,), (1,)), ((), ())), preferred_element_type=F32)


def kernel(
    na, nx, home_hbm, cluster_hbm, emb_hbm, out_ref,
    home_ref, cluster_ref, emb_ref, unit, out1, in1, in2, sib_in, kept, acc, col,
    ids1, ids1_in, ids2, ids2_in, ids3_in, ids_sib, key_ids, row_ids,
    den, den_in, den_x, ret, ret_in,
    load, send1, recv1, send2, recv2, send3, recv3,
    isend1, irecv1, isend2, irecv2, isend3, irecv3, isend4, irecv4,
    dsend1, drecv1, dsend2, drecv2, dsend3, drecv3, entered,
):
    nb = na
    nk = 2 * nb // nx
    nj = nb // nx
    half = nx // 2
    rows, feat = emb_ref.shape
    hf = feat // 2
    ns = na // 2
    nq = 2 * nx
    chunk = nb * ns * CAP
    wide = ns * CAP
    lanes = 128
    group = 4

    loads = [
        pltpu.make_async_copy(src, dst, load.at[i])
        for i, (src, dst) in enumerate(
            [(home_hbm, home_ref), (cluster_hbm, cluster_ref), (emb_hbm, emb_ref)]
        )
    ]
    for copy in loads:
        copy.start()

    shard = lax.axis_index("shard")
    x = lax.axis_index("tile")
    core = lax.rem(shard, 2)
    y = lax.rem(lax.div(shard, 2), nb)
    z = lax.div(shard, 2 * nb)
    a = z + core * (y - z)
    b = y + core * (z - y)

    def on(a_to, b_to):
        z_to = a_to + core * (b_to - a_to)
        y_to = b_to + core * (a_to - b_to)
        return (z_to * nb + y_to) * 2 + core

    sibling = (shard + 1 - 2 * core, x)

    deltas = [0, 1, na - 1, na // 2]
    for far in range(2, na // 2):
        deltas += [far, na - far]

    ahead = [on(lax.rem(a + d, na), b) for d in deltas]
    behind = [on(lax.rem(a + na - d, na), b) for d in deltas]
    ring = [on(a, i) for i in range(nb)]
    b_to = [lax.rem(x - a - half * (k // nj) + nx + na * nx, nx) + nx * (k % nj) for k in range(nk)]
    owner = [on(a, b_to[k]) for k in range(nk)]
    stays = [b_to[k] == b for k in range(nk)]
    turn = lax.rem(x - a - b + 2 * na * nx, nx)
    computes = lax.rem(turn, half) == 0
    k_self = lax.div(turn, half) * nj + lax.div(b, nx)
    k_sib = lax.div(turn, half) * nj + lax.div(a, nx)

    def either(same, local, remote):
        pl.when(same)(local)
        pl.when(jnp.logical_not(same))(remote)

    def right(j):
        return lax.rem(x + j, nx)

    def left(j):
        return lax.rem(x + nx - j, nx)

    barrier = pltpu.get_barrier_semaphore()

    def greet(device):
        pl.semaphore_signal(barrier, inc=1, device_id=device, device_id_type=MESH)

    for j in range(1, nx):
        greet((shard, right(j)))
    for t in range(1, na):
        greet((ahead[t], x))
    for i in range(nb):
        @pl.when(b != i)
        def _():
            greet((ring[i], x))
    greet(sibling)

    loads[0].wait()
    home = home_ref[...]
    named = iota((2 * na * nb, rows), 0) == home
    before = (iota((rows, rows), 0) < iota((rows, rows), 1)).astype(BF16)
    counts = jnp.dot(named.astype(BF16), before, preferred_element_type=F32)
    pos = jnp.sum(jnp.where(named, counts, 0.0), axis=0, keepdims=True).astype(I32)
    c_own = home % 2
    y_own = (home // 2) % nb
    z_own = home // (2 * nb)
    a_own = z_own + core * (y_own - z_own)
    b_own = y_own + core * (z_own - y_own)
    x_own = (a_own + b_own + half * c_own) % nx
    k_own = c_own * nj + b_own // nx
    distance = (a_own - a + na) % na
    step = jnp.zeros_like(distance)
    for t in range(1, na):
        step = jnp.where(distance == deltas[t], t, step)
    offset = (x_own - x + nx) % nx
    message = offset * na + step
    lane = k_own * CAP + pos
    slot = message * (nk * CAP) + lane
    wide_lane = offset * (nk * CAP) + lane

    loads[2].wait()
    values = emb_ref[...].astype(F32)
    unit[...] = (
        values * lax.rsqrt(jnp.sum(values * values, axis=1, keepdims=True) + 1e-06)
    ).astype(BF16)

    loads[1].wait()
    marks = (cluster_ref[...] + 1).astype(F32)
    in_step = (iota((na, rows), 0) == step).astype(BF16)
    in_lane = jnp.where(iota((lanes, rows), 0) == wide_lane, marks, 0.0)
    tags = nt_dot(in_step, in_lane.astype(BF16))
    for t in range(na):
        ids1[t] = tags[t : t + 1]

    pl.semaphore_wait(barrier, nx - 1 + na - 1 + nb - 1 + 1)
    for j in range(1, nx):
        pl.semaphore_signal(
            entered, inc=1, device_id=(shard, right(j)), device_id_type=MESH
        )

    def ids1_copy(t):
        return pltpu.make_async_remote_copy(
            src_ref=ids1.at[t], dst_ref=ids1_in.at[t],
            send_sem=isend1.at[t], recv_sem=irecv1,
            device_id=(ahead[t], x), device_id_type=MESH,
        )

    def ids2_copy(i):
        return pltpu.make_async_remote_copy(
            src_ref=ids2, dst_ref=ids2_in.at[b],
            send_sem=isend2.at[i], recv_sem=irecv2,
            device_id=(ring[i], x), device_id_type=MESH,
        )

    def ids3_copy(j):
        return pltpu.make_async_remote_copy(
            src_ref=ids2_in, dst_ref=ids3_in.at[j],
            send_sem=isend3.at[j], recv_sem=irecv3,
            device_id=(shard, right(j)), device_id_type=MESH,
        )

    def out1_copy(j, t):
        q, sub = j * 2 + t // ns, t % ns
        return pltpu.make_async_remote_copy(
            src_ref=out1.at[q, sub], dst_ref=in1.at[q, sub],
            send_sem=send1.at[j, t], recv_sem=recv1.at[q],
            device_id=(ahead[t], right(j)), device_id_type=MESH,
        )

    def place(j, h):
        q = j * 2 + h
        size = ns * nk * CAP
        pick = (iota((size, rows), 0) + q * size == slot).astype(BF16)
        placed = jnp.dot(pick, unit[...], preferred_element_type=F32)
        placed = placed.reshape(ns * nk, CAP, feat)
        placed = jnp.concatenate([placed[:, :, :hf], placed[:, :, hf:]], axis=1).astype(BF16)
        out1[q] = placed.reshape(ns, nk, 2 * CAP, hf)

    def send_stage(j, first):
        for h in range(2):
            place(j, h)
            for t in range(h * ns, (h + 1) * ns):
                if first and t == 0:
                    pltpu.make_async_copy(out1.at[0, 0], in1.at[0, 0], recv1.at[0]).start()
                else:
                    out1_copy(j, t).start()

    def sent_stage(j):
        for t in range(na):
            if t > 0:
                out1_copy(j, t).wait_send()
            else:
                @pl.when(j > 0)
                def _():
                    out1_copy(j, t).wait_send()

    def rows2_copy(q, k):
        return pltpu.make_async_remote_copy(
            src_ref=in1.at[q, :, k], dst_ref=in2.at[q, b],
            send_sem=send2.at[q, k], recv_sem=recv2.at[q],
            device_id=(owner[k], x), device_id_type=MESH,
        )

    def forward(q):
        pltpu.make_async_copy(in1.at[q], in1.at[q], recv1.at[q]).wait()
        for k in range(nk):
            either(
                stays[k],
                lambda: pltpu.make_async_copy(in1.at[q, :, k], in2.at[q, b], recv2.at[q]).start(),
                lambda: rows2_copy(q, k).start(),
            )

    def forwarded(q):
        for k in range(nk):
            @pl.when(jnp.logical_not(stays[k]))
            def _():
                rows2_copy(q, k).wait_send()

    def sib_ids_copy():
        return pltpu.make_async_remote_copy(
            src_ref=ids3_in, dst_ref=ids_sib, send_sem=isend4, recv_sem=irecv4,
            device_id=sibling, device_id_type=MESH,
        )

    def sib_rows_copy(t):
        return pltpu.make_async_remote_copy(
            src_ref=kept.at[0, t], dst_ref=sib_in.at[t],
            send_sem=send3.at[t], recv_sem=recv3.at[t],
            device_id=sibling, device_id_type=MESH,
        )

    def spread_ids(source, side, k):
        def spread(q, carry):
            j, h = lax.div(q, 2), lax.rem(q, 2)
            block = jnp.concatenate(
                [source[j, i, pl.ds(h * ns, ns), :] for i in range(nb)], axis=0
            )
            block = jnp.broadcast_to(block[:, None, :], (nb * ns, CAP, lanes))
            here = iota((nb * ns, CAP, lanes), 1) + (j * nk + k) * CAP
            block = jnp.where(iota((nb * ns, CAP, lanes), 2) == here, block, 0.0)
            block = block.reshape(chunk, lanes)
            row_ids[side, q] = jnp.broadcast_to(
                jnp.sum(block, axis=1, keepdims=True), (chunk, lanes)
            )
            key_ids[side, q] = nt_dot(jnp.ones((8, lanes), BF16), block.astype(BF16))
            return carry

        lax.fori_loop(0, nq, spread, 0)

    def tile(side, g, key_side, t, last, by_row, by_col, sums):
        left = kept[side, pl.ds(g * group, group)].reshape(group * chunk, feat)
        scores = nt_dot(left, kept[key_side, t])
        weights = jnp.exp2(scores * SCALE)
        theirs = key_ids[key_side, t, 0:1, :]
        for i in range(group):
            at = g * group + i
            mine = row_ids[side, at]
            valid = jnp.where(at <= last, theirs, -1.0)
            matched = [
                jnp.where(
                    mine == valid[:, j : j + lanes],
                    weights[i * chunk : (i + 1) * chunk, j : j + lanes],
                    0.0,
                )
                for j in range(0, chunk, lanes)
            ]
            if by_row:
                acc[at] += functools.reduce(jnp.add, matched)
            if by_col:
                parts = [jnp.sum(m.reshape(chunk // 8, 8, lanes), axis=0) for m in matched]
                part = jnp.concatenate(parts, axis=1)
                if by_row:
                    part = jnp.where(at < t, part, 0.0)
                sums += part
        return sums

    def pair_sums(t, carry):
        pltpu.make_async_copy(in2.at[t], in2.at[t], recv2.at[t]).wait()
        block = in2[t].reshape(nb * ns, 2 * CAP, hf).astype(F32)
        block = jnp.concatenate([block[:, :CAP, :], block[:, CAP:, :]], axis=2)
        kept[0, t] = block.reshape(chunk, feat).astype(BF16)
        sib_rows_copy(t).start()

        groups = lax.div(t + group, group)
        sums = lax.fori_loop(
            0, groups, lambda g, c: tile(0, g, 0, t, t, True, True, c),
            jnp.zeros((8, chunk), F32),
        )
        sib_rows_copy(t).wait_recv()
        kept[1, t] = sib_in[t]
        sums = lax.fori_loop(
            0, groups, lambda g, c: tile(1, g, 0, t, t, False, True, c), sums
        )
        col[pl.ds(t, 1), :] = jnp.sum(sums, axis=0, keepdims=True)
        lax.fori_loop(
            0, lax.div(t + group - 1, group),
            lambda g, c: tile(0, g, 1, t, t - 1, True, False, c), 0,
        )
        return carry

    pltpu.make_async_copy(ids1.at[0], ids1_in.at[0], irecv1).start()
    for t in range(1, na):
        ids1_copy(t).start()
    send_stage(0, True)
    pltpu.make_async_copy(ids1, ids1_in, irecv1).wait()
    ids2[...] = jnp.concatenate([ids1_in[t] for t in range(na)], axis=0)
    for i in range(nb):
        either(
            b == i,
            lambda: pltpu.make_async_copy(ids2, ids2_in.at[b], irecv2).start(),
            lambda: ids2_copy(i).start(),
        )
    pl.semaphore_wait(entered, nx - 1)
    send_stage(1, False)
    pltpu.make_async_copy(ids2_in, ids2_in, irecv2).wait()
    pltpu.make_async_copy(ids2_in, ids3_in.at[0], irecv3).start()
    for j in range(1, nx):
        ids3_copy(j).start()

    def stage(j, carry):
        @pl.when(j < nx)
        def _():
            for h in range(2):
                @pl.when(j >= 2)
                def _():
                    forwarded(2 * j - 4 + h)

                forward(2 * j + h)

            @pl.when(j < nx - 2)
            def _():
                sent_stage(j)
                send_stage(j + 2, False)

        @pl.when(computes & (j == 0))
        def _():
            pltpu.make_async_copy(ids3_in, ids3_in, irecv3).wait()
            sib_ids_copy().start()
            spread_ids(ids3_in, 0, k_self)
            acc[...] = jnp.zeros_like(acc)

        @pl.when(computes & (j == 1))
        def _():
            sib_ids_copy().wait_recv()
            spread_ids(ids_sib, 1, k_sib)

        @pl.when(computes & (j > 0))
        def _():
            lax.fori_loop(2 * j - 2, 2 * j, pair_sums, 0)
        return carry

    lax.fori_loop(0, nx + 1, stage, 0)

    def den1_copy(to):
        return pltpu.make_async_remote_copy(
            src_ref=den.at[to], dst_ref=den_in.at[k_self],
            send_sem=dsend1.at[to], recv_sem=drecv1,
            device_id=(ring[to], x), device_id_type=MESH,
        )

    @pl.when(computes)
    def _():
        same = iota((chunk, lanes), 1) == iota((chunk, lanes), 0) % wide
        for t in range(nq):
            sums = jnp.sum(acc[t], axis=1, keepdims=True)
            block = jnp.where(same, sums, 0.0).reshape(nb, wide, lanes)
            block = jnp.sum(block, axis=1)
            for j in range(nb):
                den[j, t : t + 1, :] = block[j : j + 1]
        by_col = col[...]
        per = lanes // wide
        for j in range(nb):
            part = by_col[:, j // per * lanes : (j // per + 1) * lanes]
            turns = (-(j % per) * wide) % lanes
            part = pltpu.roll(part, turns, 1) if turns else part
            part = jnp.where(iota((nq, lanes), 1) < wide, part, 0.0)
            den[j] = (den[j] + part) * (2.0 ** (-SCALE))
            either(
                b == j,
                lambda: pltpu.make_async_copy(den.at[j], den_in.at[k_self], drecv1).start(),
                lambda: den1_copy(j).start(),
            )

    @pl.when(jnp.logical_not(computes))
    def _():
        pltpu.make_async_copy(ids3_in, ids3_in, irecv3).wait()

    for j in range(nx - 2, nx):
        sent_stage(j)
    for i in range(1, na):
        ids1_copy(i).wait_send()
    pltpu.make_async_copy(den_in, den_in, drecv1).wait()

    def den2_copy(j):
        return pltpu.make_async_remote_copy(
            src_ref=den_in, dst_ref=den_x.at[j - 1],
            send_sem=dsend2.at[j - 1], recv_sem=drecv2,
            device_id=(shard, left(j)), device_id_type=MESH,
        )

    for j in range(1, nx):
        den2_copy(j).start()
    for q in range(2 * nx - 4, 2 * nx):
        forwarded(q)
    for i in range(nb):
        @pl.when(b != i)
        def _():
            ids2_copy(i).wait_send()
    for j in range(1, nx):
        ids3_copy(j).wait_send()
    pltpu.make_async_copy(den_x, den_x, drecv2).wait()

    def ret_copy(t):
        return pltpu.make_async_remote_copy(
            src_ref=ret.at[t], dst_ref=ret_in.at[t],
            send_sem=dsend3.at[t], recv_sem=drecv3,
            device_id=(behind[t], x), device_id_type=MESH,
        )

    at_lane = iota((2, lanes), 1)
    for sub in range(ns):
        block = jnp.zeros((2, lanes), F32)
        for j in range(nx):
            for k in range(nk):
                part = den_in[k] if j == 0 else den_x[j - 1, k]
                turns = ((j * nk + k - sub) * CAP) % lanes
                part = jnp.where(at_lane // CAP == sub, part[2 * j : 2 * j + 2], 0.0)
                block += pltpu.roll(part, turns, 1) if turns else part
        for h in range(2):
            t = h * ns + sub
            ret[t] = block[h : h + 1]
            if t > 0:
                ret_copy(t).start()
            else:
                pltpu.make_async_copy(ret.at[0], ret_in.at[0], drecv3).start()

    @pl.when(computes)
    def _():
        sib_ids_copy().wait_send()
        for q in range(nq):
            sib_rows_copy(q).wait_send()
        for i in range(nb):
            @pl.when(b != i)
            def _():
                den1_copy(i).wait_send()

    for j in range(1, nx):
        den2_copy(j).wait_send()
    chosen = (iota((lanes, rows), 0) == step).astype(BF16)
    pltpu.make_async_copy(ret, ret_in, drecv3).wait()

    table = jnp.concatenate(
        [ret_in[t] for t in range(na)] + [jnp.zeros((lanes - na, lanes), F32)], axis=0
    ).T
    high = table.astype(BF16)
    rest = table - high.astype(F32)
    mid = rest.astype(BF16)
    low = (rest - mid.astype(F32)).astype(BF16)
    picked = (
        jnp.dot(low, chosen, preferred_element_type=F32)
        + jnp.dot(mid, chosen, preferred_element_type=F32)
    ) + jnp.dot(high, chosen, preferred_element_type=F32)
    out_ref[...] = jnp.sum(
        jnp.where(iota((lanes, rows), 0) == wide_lane, picked, 0.0), axis=0, keepdims=True
    )

    for t in range(1, na):
        ret_copy(t).wait_send()


def shards(n_tile, embeddings, cluster, home):
    n_shard = lax.axis_size("shard")
    na = next(n for n in range(1, n_shard + 1) if 2 * n * n == n_shard)
    nx = n_tile
    nk = 2 * na // nx
    rows, feat = embeddings.shape
    ns = na // 2
    nq = 2 * nx
    chunk = na * ns * CAP
    hf = feat // 2
    vmem = pltpu.VMEM
    dma = pltpu.SemaphoreType.DMA
    out = pl.pallas_call(
        functools.partial(kernel, na, nx),
        out_shape=jax.ShapeDtypeStruct((1, rows), F32),
        in_specs=[pl.BlockSpec(memory_space=pl.ANY)] * 3,
        out_specs=pl.BlockSpec(memory_space=pltpu.VMEM),
        scratch_shapes=[
            vmem((1, rows), I32),
            vmem((1, rows), I32),
            vmem((rows, feat), BF16),
            vmem((rows, feat), BF16),
            vmem((nq, ns, nk, 2 * CAP, hf), BF16),
            vmem((nq, ns, nk, 2 * CAP, hf), BF16),
            vmem((nq, na, ns, 2 * CAP, hf), BF16),
            vmem((nq, chunk, feat), BF16),
            vmem((2, nq, chunk, feat), BF16),
            vmem((nq, chunk, 128), F32),
            vmem((nq, chunk), F32),
            vmem((na, 1, 128), F32),
            vmem((na, 1, 128), F32),
            vmem((na, 128), F32),
            vmem((na, na, 128), F32),
            vmem((nx, na, na, 128), F32),
            vmem((nx, na, na, 128), F32),
            vmem((2, nq, 8, chunk), F32),
            vmem((2, nq, chunk, 128), F32),
            vmem((na, nq, 128), F32),
            vmem((nk, nq, 128), F32),
            vmem((nx - 1, nk, nq, 128), F32),
            vmem((na, 1, 128), F32),
            vmem((na, 1, 128), F32),
            dma((3,)),
            dma((nx, na)), dma((nq,)), dma((nq, nk)), dma((nq,)), dma((nq,)), dma((nq,)),
            dma((na,)), dma(()), dma((na,)), dma(()), dma((nx,)), dma(()), dma(()), dma(()),
            dma((na,)), dma(()), dma((nx - 1,)), dma(()), dma((na,)), dma(()),
            pltpu.SemaphoreType.REGULAR,
        ],
        compiler_params=pltpu.CompilerParams(
            collective_id=0, has_side_effects=True, vmem_limit_bytes=48 * 2**20
        ),
    )(home.reshape(1, rows), cluster.reshape(1, rows), embeddings)
    return out.reshape(rows)


def solution(mesh):
    return jax.shard_map(
        functools.partial(shards, mesh.shape["tile"]),
        mesh=mesh,
        in_specs=(P(("shard", "tile"), None), P(("shard", "tile")), P(("shard", "tile"))),
        out_specs=P(("shard", "tile")),
        check_vma=False,
    )
```

```python
import functools

import jax
import jax.numpy as jnp
from jax import lax
from jax.experimental import pallas as pl
from jax.experimental.pallas import tpu as pltpu
from jax.sharding import PartitionSpec as P

F32 = jnp.float32
BF16 = jnp.bfloat16
I32 = jnp.int32
MESH = pl.DeviceIdType.MESH
CAP = 8
SCALE = 10.0 * 1.4426950408889634


def iota(shape, dim):
    return lax.broadcasted_iota(I32, shape, dim)


def nt_dot(left, right):
    return lax.dot_general(left, right, (((1,), (1,)), ((), ())), preferred_element_type=F32)


def kernel(
    na, nx, home_hbm, cluster_hbm, emb_hbm, out_ref,
    home_ref, cluster_ref, emb_ref, unit, out1, in1, in2, passing, sib_in, kept, acc, col,
    ids1, ids1_in, ids2, ids2_in, ids3_in, ids_sib, key_ids, row_ids,
    den, den_in, ret, ret_in,
    load, send1, recv1, send2, recv2, send3, recv3, rsend, rrecv,
    isend1, irecv1, isend2, irecv2, isend3, irecv3, isend4, irecv4,
    dsend1, drecv1, dsend2, drecv2, entered,
):
    nb = na
    nk = 2 * nb // nx
    nj = nb // nx
    half = nx // 2
    rows, feat = emb_ref.shape
    hf = feat // 2
    ns = na // 2
    nq = 2 * nx
    chunk = nb * ns * CAP
    wide = ns * CAP
    lanes = 128
    group = 4

    loads = [
        pltpu.make_async_copy(src, dst, load.at[i])
        for i, (src, dst) in enumerate(
            [(home_hbm, home_ref), (cluster_hbm, cluster_ref), (emb_hbm, emb_ref)]
        )
    ]
    for copy in loads:
        copy.start()

    shard = lax.axis_index("shard")
    x = lax.axis_index("tile")
    core = lax.rem(shard, 2)
    y = lax.rem(lax.div(shard, 2), nb)
    z = lax.div(shard, 2 * nb)
    a = z + core * (y - z)
    b = y + core * (z - y)

    def on(a_to, b_to):
        z_to = a_to + core * (b_to - a_to)
        y_to = b_to + core * (a_to - b_to)
        return (z_to * nb + y_to) * 2 + core

    sibling = (shard + 1 - 2 * core, x)

    deltas = [0, 1, na - 1, na // 2]
    for far in range(2, na // 2):
        deltas += [far, na - far]

    ahead = [on(lax.rem(a + d, na), b) for d in deltas]
    behind = [on(lax.rem(a + na - d, na), b) for d in deltas]
    ring = [on(a, i) for i in range(nb)]
    b_to = [lax.rem(x - a - half * (k // nj) + nx + na * nx, nx) + nx * (k % nj) for k in range(nk)]
    owner = [on(a, b_to[k]) for k in range(nk)]
    stays = [b_to[k] == b for k in range(nk)]
    turn = lax.rem(x - a - b + 2 * na * nx, nx)
    computes = lax.rem(turn, half) == 0
    k_self = lax.div(turn, half) * nj + lax.div(b, nx)
    k_sib = lax.div(turn, half) * nj + lax.div(a, nx)

    opposite = [computes & (b_to[k] == lax.rem(b + nb // 2, nb)) for k in range(nk)]
    turned = 1 - 2 * lax.rem(b, 2)
    relay = on(a, lax.rem(b - turned + nb, nb))
    relay_from = lax.rem(b - turned + nb, nb)
    relay_to = on(a, lax.rem(b + (nb // 2 - 1) * turned + nb, nb))

    def either(same, local, remote):
        pl.when(same)(local)
        pl.when(jnp.logical_not(same))(remote)

    def right(j):
        return lax.rem(x + j, nx)

    def left(j):
        return lax.rem(x + nx - j, nx)

    barrier = pltpu.get_barrier_semaphore()

    def greet(device):
        pl.semaphore_signal(barrier, inc=1, device_id=device, device_id_type=MESH)

    for j in range(1, nx):
        greet((shard, right(j)))
    for t in range(1, na):
        greet((ahead[t], x))
    for i in range(nb):
        @pl.when(b != i)
        def _():
            greet((ring[i], x))
    greet(sibling)

    loads[0].wait()
    home = home_ref[...]
    named = iota((2 * na * nb, rows), 0) == home
    before = (iota((rows, rows), 0) < iota((rows, rows), 1)).astype(BF16)
    counts = jnp.dot(named.astype(BF16), before, preferred_element_type=F32)
    pos = jnp.sum(jnp.where(named, counts, 0.0), axis=0, keepdims=True).astype(I32)
    c_own = home % 2
    y_own = (home // 2) % nb
    z_own = home // (2 * nb)
    a_own = z_own + core * (y_own - z_own)
    b_own = y_own + core * (z_own - y_own)
    x_own = (a_own + b_own + half * c_own) % nx
    k_own = c_own * nj + b_own // nx
    distance = (a_own - a + na) % na
    step = jnp.zeros_like(distance)
    for t in range(1, na):
        step = jnp.where(distance == deltas[t], t, step)
    offset = (x_own - x + nx) % nx
    message = offset * na + step
    lane = k_own * CAP + pos
    slot = message * (nk * CAP) + lane
    wide_lane = offset * (nk * CAP) + lane

    loads[2].wait()
    values = emb_ref[...].astype(F32)
    unit[...] = (
        values * lax.rsqrt(jnp.sum(values * values, axis=1, keepdims=True) + 1e-06)
    ).astype(BF16)

    loads[1].wait()
    marks = (cluster_ref[...] + 1).astype(F32)
    in_step = (iota((na, rows), 0) == step).astype(BF16)
    in_lane = jnp.where(iota((lanes, rows), 0) == wide_lane, marks, 0.0)
    tags = nt_dot(in_step, in_lane.astype(BF16))
    for t in range(na):
        ids1[t] = tags[t : t + 1]

    pl.semaphore_wait(barrier, nx - 1 + na - 1 + nb - 1 + 1)
    for j in range(1, nx):
        pl.semaphore_signal(
            entered, inc=1, device_id=(shard, right(j)), device_id_type=MESH
        )

    def ids1_copy(t):
        return pltpu.make_async_remote_copy(
            src_ref=ids1.at[t], dst_ref=ids1_in.at[t],
            send_sem=isend1.at[t], recv_sem=irecv1,
            device_id=(ahead[t], x), device_id_type=MESH,
        )

    def ids2_copy(i):
        return pltpu.make_async_remote_copy(
            src_ref=ids2, dst_ref=ids2_in.at[b],
            send_sem=isend2.at[i], recv_sem=irecv2,
            device_id=(ring[i], x), device_id_type=MESH,
        )

    def ids3_copy(j):
        return pltpu.make_async_remote_copy(
            src_ref=ids2_in, dst_ref=ids3_in.at[j],
            send_sem=isend3.at[j], recv_sem=irecv3,
            device_id=(shard, right(j)), device_id_type=MESH,
        )

    def out1_copy(j, t):
        q, sub = j * 2 + t // ns, t % ns
        return pltpu.make_async_remote_copy(
            src_ref=out1.at[q, sub], dst_ref=in1.at[q, sub],
            send_sem=send1.at[j, t], recv_sem=recv1.at[q],
            device_id=(ahead[t], right(j)), device_id_type=MESH,
        )

    def place(j, h):
        q = j * 2 + h
        size = ns * nk * CAP
        pick = (iota((size, rows), 0) + q * size == slot).astype(BF16)
        placed = jnp.dot(pick, unit[...], preferred_element_type=F32)
        placed = placed.reshape(ns * nk, CAP, feat)
        placed = jnp.concatenate([placed[:, :, :hf], placed[:, :, hf:]], axis=1).astype(BF16)
        out1[q] = placed.reshape(ns, nk, 2 * CAP, hf)

    def send_stage(j, first):
        for h in range(2):
            place(j, h)
            for t in range(h * ns, (h + 1) * ns):
                if first and t == 0:
                    pltpu.make_async_copy(out1.at[0, 0], in1.at[0, 0], recv1.at[0]).start()
                else:
                    out1_copy(j, t).start()

    def sent_stage(j):
        for t in range(na):
            if t > 0:
                out1_copy(j, t).wait_send()
            else:
                @pl.when(j > 0)
                def _():
                    out1_copy(j, t).wait_send()

    def rows2_copy(q, k):
        return pltpu.make_async_remote_copy(
            src_ref=in1.at[q, :, k], dst_ref=in2.at[q, b],
            send_sem=send2.at[q, k], recv_sem=recv2.at[q],
            device_id=(owner[k], x), device_id_type=MESH,
        )

    def forward(j, h):
        q = 2 * j + h
        pltpu.make_async_copy(in1.at[q], in1.at[q], recv1.at[q]).wait()
        for k in range(nk):
            def away(k=k):
                if h == 0:
                    rows2_copy(q, k).start()
                else:
                    either(
                        opposite[k],
                        lambda: relay_copy(j, k).start(),
                        lambda: rows2_copy(q, k).start(),
                    )

            either(
                stays[k],
                lambda: pltpu.make_async_copy(in1.at[q, :, k], in2.at[q, b], recv2.at[q]).start(),
                away,
            )

    def relay_copy(j, k):
        return pltpu.make_async_remote_copy(
            src_ref=in1.at[2 * j + 1, :, k], dst_ref=passing.at[j],
            send_sem=send2.at[2 * j + 1, k], recv_sem=rrecv.at[j],
            device_id=(relay, x), device_id_type=MESH,
        )

    def passed_copy(j):
        return pltpu.make_async_remote_copy(
            src_ref=passing.at[j], dst_ref=in2.at[2 * j + 1, relay_from],
            send_sem=rsend.at[j], recv_sem=recv2.at[2 * j + 1],
            device_id=(relay_to, x), device_id_type=MESH,
        )

    def forwarded(q):
        for k in range(nk):
            @pl.when(jnp.logical_not(stays[k]))
            def _():
                rows2_copy(q, k).wait_send()

    def sib_ids_copy():
        return pltpu.make_async_remote_copy(
            src_ref=ids3_in, dst_ref=ids_sib, send_sem=isend4, recv_sem=irecv4,
            device_id=sibling, device_id_type=MESH,
        )

    def sib_rows_copy(t):
        return pltpu.make_async_remote_copy(
            src_ref=kept.at[0, t], dst_ref=sib_in.at[t],
            send_sem=send3.at[t], recv_sem=recv3.at[t],
            device_id=sibling, device_id_type=MESH,
        )

    def spread_ids(source, side, k):
        def spread(q, carry):
            j, h = lax.div(q, 2), lax.rem(q, 2)
            block = jnp.concatenate(
                [source[j, i, pl.ds(h * ns, ns), :] for i in range(nb)], axis=0
            )
            block = jnp.broadcast_to(block[:, None, :], (nb * ns, CAP, lanes))
            here = iota((nb * ns, CAP, lanes), 1) + (j * nk + k) * CAP
            block = jnp.where(iota((nb * ns, CAP, lanes), 2) == here, block, 0.0)
            block = block.reshape(chunk, lanes)
            row_ids[side, q] = jnp.broadcast_to(
                jnp.sum(block, axis=1, keepdims=True), (chunk, lanes)
            )
            key_ids[side, q] = nt_dot(jnp.ones((8, lanes), BF16), block.astype(BF16))
            return carry

        lax.fori_loop(0, nq, spread, 0)

    def tile(side, g, key_side, t, last, by_row, by_col, sums):
        left = kept[side, pl.ds(g * group, group)].reshape(group * chunk, feat)
        scores = nt_dot(left, kept[key_side, t])
        weights = jnp.exp2(scores * SCALE)
        theirs = key_ids[key_side, t, 0:1, :]
        for i in range(group):
            at = g * group + i
            mine = row_ids[side, at]
            valid = jnp.where(at <= last, theirs, -1.0)
            matched = [
                jnp.where(
                    mine == valid[:, j : j + lanes],
                    weights[i * chunk : (i + 1) * chunk, j : j + lanes],
                    0.0,
                )
                for j in range(0, chunk, lanes)
            ]
            if by_row:
                acc[at] += functools.reduce(jnp.add, matched)
            if by_col:
                parts = [jnp.sum(m.reshape(chunk // 8, 8, lanes), axis=0) for m in matched]
                part = jnp.concatenate(parts, axis=1)
                if by_row:
                    part = jnp.where(at < t, part, 0.0)
                sums += part
        return sums

    def pair_sums(t, carry):
        pltpu.make_async_copy(in2.at[t], in2.at[t], recv2.at[t]).wait()
        block = in2[t].reshape(nb * ns, 2 * CAP, hf).astype(F32)
        block = jnp.concatenate([block[:, :CAP, :], block[:, CAP:, :]], axis=2)
        kept[0, t] = block.reshape(chunk, feat).astype(BF16)
        sib_rows_copy(t).start()

        groups = lax.div(t + group, group)
        sums = lax.fori_loop(
            0, groups, lambda g, c: tile(0, g, 0, t, t, True, True, c),
            jnp.zeros((8, chunk), F32),
        )
        sib_rows_copy(t).wait_recv()
        kept[1, t] = sib_in[t]
        sums = lax.fori_loop(
            0, groups, lambda g, c: tile(1, g, 0, t, t, False, True, c), sums
        )
        col[pl.ds(t, 1), :] = jnp.sum(sums, axis=0, keepdims=True)
        lax.fori_loop(
            0, lax.div(t + group - 1, group),
            lambda g, c: tile(0, g, 1, t, t - 1, True, False, c), 0,
        )
        return carry

    pltpu.make_async_copy(ids1.at[0], ids1_in.at[0], irecv1).start()
    for t in range(1, na):
        ids1_copy(t).start()
    send_stage(0, True)
    pltpu.make_async_copy(ids1, ids1_in, irecv1).wait()
    ids2[...] = jnp.concatenate([ids1_in[t] for t in range(na)], axis=0)
    for i in range(nb):
        either(
            b == i,
            lambda: pltpu.make_async_copy(ids2, ids2_in.at[b], irecv2).start(),
            lambda: ids2_copy(i).start(),
        )
    pl.semaphore_wait(entered, nx - 1)
    send_stage(1, False)
    pltpu.make_async_copy(ids2_in, ids2_in, irecv2).wait()
    pltpu.make_async_copy(ids2_in, ids3_in.at[0], irecv3).start()
    for j in range(1, nx):
        ids3_copy(j).start()

    def stage(j, carry):
        @pl.when(j < nx)
        def _():
            for h in range(2):
                @pl.when(j >= 2)
                def _():
                    forwarded(2 * j - 4 + h)

                forward(j, h)

            @pl.when(j < nx - 2)
            def _():
                sent_stage(j)
                send_stage(j + 2, False)

            @pl.when(jnp.logical_not(computes))
            def _():
                pltpu.make_async_copy(passing.at[j], passing.at[j], rrecv.at[j]).wait()
                passed_copy(j).start()

        @pl.when(computes & (j == 0))
        def _():
            pltpu.make_async_copy(ids3_in, ids3_in, irecv3).wait()
            sib_ids_copy().start()
            spread_ids(ids3_in, 0, k_self)
            acc[...] = jnp.zeros_like(acc)

        @pl.when(computes & (j == 1))
        def _():
            sib_ids_copy().wait_recv()
            spread_ids(ids_sib, 1, k_sib)

        @pl.when(computes & (j > 0))
        def _():
            lax.fori_loop(2 * j - 2, 2 * j, pair_sums, 0)
        return carry

    lax.fori_loop(0, nx + 1, stage, 0)

    def den1_copy(to):
        return pltpu.make_async_remote_copy(
            src_ref=den.at[to], dst_ref=den_in.at[k_self],
            send_sem=dsend1.at[to], recv_sem=drecv1,
            device_id=(ring[to], x), device_id_type=MESH,
        )

    @pl.when(computes)
    def _():
        same = iota((chunk, lanes), 1) == iota((chunk, lanes), 0) % wide
        for t in range(nq):
            sums = jnp.sum(acc[t], axis=1, keepdims=True)
            block = jnp.where(same, sums, 0.0).reshape(nb, wide, lanes)
            block = jnp.sum(block, axis=1)
            for j in range(nb):
                den[j, t : t + 1, :] = block[j : j + 1]
        by_col = col[...]
        per = lanes // wide
        for j in range(nb):
            part = by_col[:, j // per * lanes : (j // per + 1) * lanes]
            turns = (-(j % per) * wide) % lanes
            part = pltpu.roll(part, turns, 1) if turns else part
            part = jnp.where(iota((nq, lanes), 1) < wide, part, 0.0)
            den[j] = (den[j] + part) * (2.0 ** (-SCALE))
            either(
                b == j,
                lambda: pltpu.make_async_copy(den.at[j], den_in.at[k_self], drecv1).start(),
                lambda: den1_copy(j).start(),
            )

    @pl.when(jnp.logical_not(computes))
    def _():
        pltpu.make_async_copy(ids3_in, ids3_in, irecv3).wait()
        for j in range(nx):
            passed_copy(j).wait_send()

    for j in range(nx - 2, nx):
        sent_stage(j)
    at_lane = iota((nq, lanes), 1)
    in_place = [at_lane // CAP == sub for sub in range(ns)]
    pltpu.make_async_copy(den_in, den_in, drecv1).wait()

    def ret_copy(q, sub):
        return pltpu.make_async_remote_copy(
            src_ref=ret.at[q * ns + sub], dst_ref=ret_in.at[q * ns + sub],
            send_sem=dsend2.at[q, sub], recv_sem=drecv2,
            device_id=(behind[q % 2 * ns + sub], left(q // 2)), device_id_type=MESH,
        )

    for sub in range(ns):
        block = jnp.zeros((nq, lanes), F32)
        for k in range(nk):
            part = jnp.where(in_place[sub], den_in[k], 0.0)
            turns = ((k - sub) * CAP) % lanes
            block += pltpu.roll(part, turns, 1) if turns else part
        for q in range(nq):
            ret[q * ns + sub] = block[q : q + 1]
            if q + sub > 0:
                ret_copy(q, sub).start()
            else:
                pltpu.make_async_copy(ret.at[0], ret_in.at[0], drecv2).start()

    for i in range(1, na):
        ids1_copy(i).wait_send()
    for i in range(nb):
        @pl.when(b != i)
        def _():
            ids2_copy(i).wait_send()
    for j in range(1, nx):
        ids3_copy(j).wait_send()
    for q in range(2 * nx - 4, 2 * nx):
        forwarded(q)

    @pl.when(computes)
    def _():
        sib_ids_copy().wait_send()
        for q in range(nq):
            sib_rows_copy(q).wait_send()
        for i in range(nb):
            @pl.when(b != i)
            def _():
                den1_copy(i).wait_send()

    chosen = (iota((lanes, rows), 0) == message).astype(BF16)
    pltpu.make_async_copy(ret, ret_in, drecv2).wait()

    table = jnp.concatenate(
        [ret_in[m] for m in range(na * nx)] + [jnp.zeros((lanes - na * nx, lanes), F32)], axis=0
    )
    table = table.T[: nk * CAP]
    high = table.astype(BF16)
    rest = table - high.astype(F32)
    mid = rest.astype(BF16)
    low = (rest - mid.astype(F32)).astype(BF16)
    picked = (
        jnp.dot(low, chosen, preferred_element_type=F32)
        + jnp.dot(mid, chosen, preferred_element_type=F32)
    ) + jnp.dot(high, chosen, preferred_element_type=F32)
    out_ref[...] = jnp.sum(
        jnp.where(iota((nk * CAP, rows), 0) == lane, picked, 0.0), axis=0, keepdims=True
    )

    for q in range(nq):
        for sub in range(ns):
            if q + sub > 0:
                ret_copy(q, sub).wait_send()


def shards(n_tile, embeddings, cluster, home):
    n_shard = lax.axis_size("shard")
    na = next(n for n in range(1, n_shard + 1) if 2 * n * n == n_shard)
    nx = n_tile
    nk = 2 * na // nx
    rows, feat = embeddings.shape
    ns = na // 2
    nq = 2 * nx
    chunk = na * ns * CAP
    hf = feat // 2
    vmem = pltpu.VMEM
    dma = pltpu.SemaphoreType.DMA
    out = pl.pallas_call(
        functools.partial(kernel, na, nx),
        out_shape=jax.ShapeDtypeStruct((1, rows), F32),
        in_specs=[pl.BlockSpec(memory_space=pl.ANY)] * 3,
        out_specs=pl.BlockSpec(memory_space=pltpu.VMEM),
        scratch_shapes=[
            vmem((1, rows), I32),
            vmem((1, rows), I32),
            vmem((rows, feat), BF16),
            vmem((rows, feat), BF16),
            vmem((nq, ns, nk, 2 * CAP, hf), BF16),
            vmem((nq, ns, nk, 2 * CAP, hf), BF16),
            vmem((nq, na, ns, 2 * CAP, hf), BF16),
            vmem((nx, ns, 2 * CAP, hf), BF16),
            vmem((nq, chunk, feat), BF16),
            vmem((2, nq, chunk, feat), BF16),
            vmem((nq, chunk, 128), F32),
            vmem((nq, chunk), F32),
            vmem((na, 1, 128), F32),
            vmem((na, 1, 128), F32),
            vmem((na, 128), F32),
            vmem((na, na, 128), F32),
            vmem((nx, na, na, 128), F32),
            vmem((nx, na, na, 128), F32),
            vmem((2, nq, 8, chunk), F32),
            vmem((2, nq, chunk, 128), F32),
            vmem((na, nq, 128), F32),
            vmem((nk, nq, 128), F32),
            vmem((na * nx, 1, 128), F32),
            vmem((na * nx, 1, 128), F32),
            dma((3,)),
            dma((nx, na)), dma((nq,)), dma((nq, nk)), dma((nq,)), dma((nq,)), dma((nq,)),
            dma((nx,)), dma((nx,)),
            dma((na,)), dma(()), dma((na,)), dma(()), dma((nx,)), dma(()), dma(()), dma(()),
            dma((na,)), dma(()), dma((nq, ns)), dma(()), pltpu.SemaphoreType.REGULAR,
        ],
        compiler_params=pltpu.CompilerParams(
            collective_id=0, has_side_effects=True, vmem_limit_bytes=48 * 2**20
        ),
    )(home.reshape(1, rows), cluster.reshape(1, rows), embeddings)
    return out.reshape(rows)


def solution(mesh):
    return jax.shard_map(
        functools.partial(shards, mesh.shape["tile"]),
        mesh=mesh,
        in_specs=(P(("shard", "tile"), None), P(("shard", "tile")), P(("shard", "tile"))),
        out_specs=P(("shard", "tile")),
        check_vma=False,
    )
```

```python
import functools

import jax
import jax.numpy as jnp
from jax import lax
from jax.experimental import pallas as pl
from jax.experimental.pallas import tpu as pltpu
from jax.sharding import PartitionSpec as P

F32 = jnp.float32
BF16 = jnp.bfloat16
I32 = jnp.int32
MESH = pl.DeviceIdType.MESH
CAP = 8
SCALE = 10.0 * 1.4426950408889634


def iota(shape, dim):
    return lax.broadcasted_iota(I32, shape, dim)


def nt_dot(left, right):
    return lax.dot_general(left, right, (((1,), (1,)), ((), ())), preferred_element_type=F32)


def kernel(
    na, nx, home_hbm, cluster_hbm, emb_hbm, out_ref,
    home_ref, cluster_ref, emb_ref, unit, out1, in1, in2, passing, sib_in, kept, acc, col, col_part,
    ids1, ids1_in, ids2, ids2_in, ids3_in, ids_sib, key_ids, row_ids,
    den, den_in, ret, ret_in,
    load, send1, recv1, send2, recv2, send3, recv3, rsend, rrecv,
    isend1, irecv1, isend2, irecv2, isend3, irecv3, isend4, irecv4,
    dsend1, drecv1, dsend2, drecv2, entered,
):
    nb = na
    nk = 2 * nb // nx
    nj = nb // nx
    half = nx // 2
    rows, feat = emb_ref.shape
    hf = feat // 2
    ns = na // 2
    nq = 2 * nx
    chunk = nb * ns * CAP
    wide = ns * CAP
    lanes = 128

    loads = [
        pltpu.make_async_copy(src, dst, load.at[i])
        for i, (src, dst) in enumerate(
            [(home_hbm, home_ref), (cluster_hbm, cluster_ref), (emb_hbm, emb_ref)]
        )
    ]
    for copy in loads:
        copy.start()

    shard = lax.axis_index("shard")
    x = lax.axis_index("tile")
    core = lax.rem(shard, 2)
    y = lax.rem(lax.div(shard, 2), nb)
    z = lax.div(shard, 2 * nb)
    a = z + core * (y - z)
    b = y + core * (z - y)

    def on(a_to, b_to):
        z_to = a_to + core * (b_to - a_to)
        y_to = b_to + core * (a_to - b_to)
        return (z_to * nb + y_to) * 2 + core

    sibling = (shard + 1 - 2 * core, x)

    deltas = [0, 1, na - 1, na // 2]
    for far in range(2, na // 2):
        deltas += [far, na - far]

    ahead = [on(lax.rem(a + d, na), b) for d in deltas]
    behind = [on(lax.rem(a + na - d, na), b) for d in deltas]
    ring = [on(a, i) for i in range(nb)]
    b_to = [lax.rem(x - a - half * (k // nj) + nx + na * nx, nx) + nx * (k % nj) for k in range(nk)]
    owner = [on(a, b_to[k]) for k in range(nk)]
    stays = [b_to[k] == b for k in range(nk)]
    turn = lax.rem(x - a - b + 2 * na * nx, nx)
    computes = lax.rem(turn, half) == 0
    k_self = lax.div(turn, half) * nj + lax.div(b, nx)
    k_sib = lax.div(turn, half) * nj + lax.div(a, nx)

    opposite = [computes & (b_to[k] == lax.rem(b + nb // 2, nb)) for k in range(nk)]
    turned = 1 - 2 * lax.rem(b, 2)
    relay = on(a, lax.rem(b - turned + nb, nb))
    relay_from = lax.rem(b - turned + nb, nb)
    relay_to = on(a, lax.rem(b + (nb // 2 - 1) * turned + nb, nb))

    def either(same, local, remote):
        pl.when(same)(local)
        pl.when(jnp.logical_not(same))(remote)

    def right(j):
        return lax.rem(x + j, nx)

    def left(j):
        return lax.rem(x + nx - j, nx)

    barrier = pltpu.get_barrier_semaphore()

    def greet(device):
        pl.semaphore_signal(barrier, inc=1, device_id=device, device_id_type=MESH)

    for j in range(1, nx):
        greet((shard, right(j)))
    for t in range(1, na):
        greet((ahead[t], x))
    for i in range(nb):
        @pl.when(b != i)
        def _():
            greet((ring[i], x))
    greet(sibling)

    loads[0].wait()
    home = home_ref[...]
    named = iota((2 * na * nb, rows), 0) == home
    before = (iota((rows, rows), 0) < iota((rows, rows), 1)).astype(BF16)
    counts = jnp.dot(named.astype(BF16), before, preferred_element_type=F32)
    pos = jnp.sum(jnp.where(named, counts, 0.0), axis=0, keepdims=True).astype(I32)
    c_own = home % 2
    y_own = (home // 2) % nb
    z_own = home // (2 * nb)
    a_own = z_own + core * (y_own - z_own)
    b_own = y_own + core * (z_own - y_own)
    x_own = (a_own + b_own + half * c_own) % nx
    k_own = c_own * nj + b_own // nx
    distance = (a_own - a + na) % na
    step = jnp.zeros_like(distance)
    for t in range(1, na):
        step = jnp.where(distance == deltas[t], t, step)
    offset = (x_own - x + nx) % nx
    message = offset * na + step
    lane = k_own * CAP + pos
    slot = message * (nk * CAP) + lane
    wide_lane = offset * (nk * CAP) + lane

    loads[2].wait()
    values = emb_ref[...].astype(F32)
    unit[...] = (
        values * lax.rsqrt(jnp.sum(values * values, axis=1, keepdims=True) + 1e-06)
    ).astype(BF16)

    loads[1].wait()
    marks = (cluster_ref[...] + 1).astype(F32)
    in_step = (iota((na, rows), 0) == step).astype(BF16)
    in_lane = jnp.where(iota((lanes, rows), 0) == wide_lane, marks, 0.0)
    tags = nt_dot(in_step, in_lane.astype(BF16))
    for t in range(na):
        ids1[t] = tags[t : t + 1]

    def place(j, h):
        q = j * 2 + h
        size = ns * nk * CAP
        pick = (iota((size, rows), 0) + q * size == slot).astype(BF16)
        placed = jnp.dot(pick, unit[...], preferred_element_type=F32)
        placed = placed.reshape(ns * nk, CAP, feat)
        placed = jnp.concatenate([placed[:, :, :hf], placed[:, :, hf:]], axis=1).astype(BF16)
        out1[q] = placed.reshape(ns, nk, 2 * CAP, hf)

    for h in range(2):
        place(0, h)

    pl.semaphore_wait(barrier, nx - 1 + na - 1 + nb - 1 + 1)
    for j in range(1, nx):
        pl.semaphore_signal(
            entered, inc=1, device_id=(shard, right(j)), device_id_type=MESH
        )

    def ids1_copy(t):
        return pltpu.make_async_remote_copy(
            src_ref=ids1.at[t], dst_ref=ids1_in.at[t],
            send_sem=isend1.at[t], recv_sem=irecv1,
            device_id=(ahead[t], x), device_id_type=MESH,
        )

    def ids2_copy(i):
        return pltpu.make_async_remote_copy(
            src_ref=ids2, dst_ref=ids2_in.at[b],
            send_sem=isend2.at[i], recv_sem=irecv2,
            device_id=(ring[i], x), device_id_type=MESH,
        )

    def ids3_copy(j):
        return pltpu.make_async_remote_copy(
            src_ref=ids2_in, dst_ref=ids3_in.at[j],
            send_sem=isend3.at[j], recv_sem=irecv3,
            device_id=(shard, right(j)), device_id_type=MESH,
        )

    def out1_copy(j, t):
        q, sub = j * 2 + t // ns, t % ns
        return pltpu.make_async_remote_copy(
            src_ref=out1.at[q, sub], dst_ref=in1.at[q, sub],
            send_sem=send1.at[j, t], recv_sem=recv1.at[q],
            device_id=(ahead[t], right(j)), device_id_type=MESH,
        )

    def send_stage(j, first):
        for h in range(2):
            if not first:
                place(j, h)
            for t in range(h * ns, (h + 1) * ns):
                if first and t == 0:
                    pltpu.make_async_copy(out1.at[0, 0], in1.at[0, 0], recv1.at[0]).start()
                else:
                    out1_copy(j, t).start()

    def sent_stage(j):
        for t in range(na):
            if t > 0:
                out1_copy(j, t).wait_send()
            else:
                @pl.when(j > 0)
                def _():
                    out1_copy(j, t).wait_send()

    def rows2_copy(q, k):
        return pltpu.make_async_remote_copy(
            src_ref=in1.at[q, :, k], dst_ref=in2.at[q, b],
            send_sem=send2.at[q, k], recv_sem=recv2.at[q],
            device_id=(owner[k], x), device_id_type=MESH,
        )

    def forward(j, h):
        q = 2 * j + h
        pltpu.make_async_copy(in1.at[q], in1.at[q], recv1.at[q]).wait()
        for k in range(nk):
            def away(k=k):
                if h == 0:
                    rows2_copy(q, k).start()
                else:
                    either(
                        opposite[k],
                        lambda: relay_copy(j, k).start(),
                        lambda: rows2_copy(q, k).start(),
                    )

            either(
                stays[k],
                lambda: pltpu.make_async_copy(in1.at[q, :, k], in2.at[q, b], recv2.at[q]).start(),
                away,
            )

    def relay_copy(j, k):
        return pltpu.make_async_remote_copy(
            src_ref=in1.at[2 * j + 1, :, k], dst_ref=passing.at[j],
            send_sem=send2.at[2 * j + 1, k], recv_sem=rrecv.at[j],
            device_id=(relay, x), device_id_type=MESH,
        )

    def passed_copy(j):
        return pltpu.make_async_remote_copy(
            src_ref=passing.at[j], dst_ref=in2.at[2 * j + 1, relay_from],
            send_sem=rsend.at[j], recv_sem=recv2.at[2 * j + 1],
            device_id=(relay_to, x), device_id_type=MESH,
        )

    def forwarded(q):
        for k in range(nk):
            @pl.when(jnp.logical_not(stays[k]))
            def _():
                rows2_copy(q, k).wait_send()

    def sib_ids_copy():
        return pltpu.make_async_remote_copy(
            src_ref=ids3_in, dst_ref=ids_sib, send_sem=isend4, recv_sem=irecv4,
            device_id=sibling, device_id_type=MESH,
        )

    def sib_rows_copy(t):
        return pltpu.make_async_remote_copy(
            src_ref=kept.at[0, t], dst_ref=sib_in.at[t],
            send_sem=send3.at[t], recv_sem=recv3.at[t],
            device_id=sibling, device_id_type=MESH,
        )

    def spread_ids(source, side, k):
        def spread(q, carry):
            j, h = lax.div(q, 2), lax.rem(q, 2)
            block = jnp.concatenate(
                [source[j, i, pl.ds(h * ns, ns), :] for i in range(nb)], axis=0
            )
            block = jnp.broadcast_to(block[:, None, :], (nb * ns, CAP, lanes))
            here = iota((nb * ns, CAP, lanes), 1) + (j * nk + k) * CAP
            block = jnp.where(iota((nb * ns, CAP, lanes), 2) == here, block, 0.0)
            block = block.reshape(chunk, lanes)
            row_ids[side, q] = jnp.broadcast_to(
                jnp.sum(block, axis=1, keepdims=True), (chunk, lanes)
            )
            key_ids[side, q] = nt_dot(jnp.ones((8, lanes), BF16), block.astype(BF16))
            return carry

        lax.fori_loop(0, nq, spread, 0)

    def tile(size, side, key_side, t, last, by_row, by_col):
        left = kept[side, :size].reshape(size * chunk, feat)
        scores = nt_dot(left, kept[key_side, t])
        weights = jnp.exp2(scores * SCALE)
        theirs = key_ids[key_side, t, 0:1, :]
        sums = jnp.zeros((8, chunk), F32)
        for at in range(size):
            mine = row_ids[side, at]
            valid = jnp.where(at <= last, theirs, -1.0)
            matched = [
                jnp.where(
                    mine == valid[:, j : j + lanes],
                    weights[at * chunk : (at + 1) * chunk, j : j + lanes],
                    0.0,
                )
                for j in range(0, chunk, lanes)
            ]
            if by_row:
                acc[at] += functools.reduce(jnp.add, matched)
            if by_col:
                parts = [jnp.sum(m.reshape(chunk // 8, 8, lanes), axis=0) for m in matched]
                part = jnp.concatenate(parts, axis=1)
                if by_row:
                    part = jnp.where(at < t, part, 0.0)
                sums += part
        if by_col:
            col_part[...] += sums

    def strip(side, key_side, t, last, by_row, by_col):
        either(
            last < nq // 2,
            lambda: tile(nq // 2, side, key_side, t, last, by_row, by_col),
            lambda: tile(nq, side, key_side, t, last, by_row, by_col),
        )

    def pair_sums(t, carry):
        pltpu.make_async_copy(in2.at[t], in2.at[t], recv2.at[t]).wait()
        block = in2[t].reshape(nb * ns, 2 * CAP, hf).astype(F32)
        block = jnp.concatenate([block[:, :CAP, :], block[:, CAP:, :]], axis=2)
        kept[0, t] = block.reshape(chunk, feat).astype(BF16)
        sib_rows_copy(t).start()

        col_part[...] = jnp.zeros_like(col_part)
        strip(0, 0, t, t, True, True)
        sib_rows_copy(t).wait_recv()
        kept[1, t] = sib_in[t]
        strip(1, 0, t, t, False, True)
        col[pl.ds(t, 1), :] = jnp.sum(col_part[...], axis=0, keepdims=True)
        pl.when(t > 0)(lambda: strip(0, 1, t, t - 1, True, False))
        return carry

    pltpu.make_async_copy(ids1.at[0], ids1_in.at[0], irecv1).start()
    for t in range(1, na):
        ids1_copy(t).start()
    send_stage(0, True)
    pltpu.make_async_copy(ids1, ids1_in, irecv1).wait()
    ids2[...] = jnp.concatenate([ids1_in[t] for t in range(na)], axis=0)
    for i in range(nb):
        either(
            b == i,
            lambda: pltpu.make_async_copy(ids2, ids2_in.at[b], irecv2).start(),
            lambda: ids2_copy(i).start(),
        )
    pl.semaphore_wait(entered, nx - 1)
    send_stage(1, False)

    def stage(j, carry):
        @pl.when(j < nx)
        def _():
            for h in range(2):
                @pl.when(j >= 2)
                def _():
                    forwarded(2 * j - 4 + h)

                forward(j, h)

            @pl.when(j == 0)
            def _():
                pltpu.make_async_copy(ids2_in, ids2_in, irecv2).wait()
                pltpu.make_async_copy(ids2_in, ids3_in.at[0], irecv3).start()
                for i in range(1, nx):
                    ids3_copy(i).start()

            @pl.when(j < nx - 2)
            def _():
                sent_stage(j)
                send_stage(j + 2, False)

            @pl.when(jnp.logical_not(computes))
            def _():
                pltpu.make_async_copy(passing.at[j], passing.at[j], rrecv.at[j]).wait()
                passed_copy(j).start()

        @pl.when(computes & (j == 1))
        def _():
            pltpu.make_async_copy(ids3_in, ids3_in, irecv3).wait()
            sib_ids_copy().start()
            spread_ids(ids3_in, 0, k_self)
            acc[...] = jnp.zeros_like(acc)
            sib_ids_copy().wait_recv()
            spread_ids(ids_sib, 1, k_sib)

        @pl.when(computes & (j > 0))
        def _():
            lax.fori_loop(2 * j - 2, 2 * j, pair_sums, 0)
        return carry

    lax.fori_loop(0, nx + 1, stage, 0)

    def den1_copy(to, u):
        return pltpu.make_async_remote_copy(
            src_ref=den.at[to], dst_ref=den_in.at[u, k_self],
            send_sem=dsend1.at[to, u], recv_sem=drecv1,
            device_id=(ring[to], left(2 * u)), device_id_type=MESH,
        )

    @pl.when(computes)
    def _():
        same = iota((chunk, lanes), 1) == iota((chunk, lanes), 0) % wide
        for t in range(nq):
            sums = jnp.sum(acc[t], axis=1, keepdims=True)
            block = jnp.where(same, sums, 0.0).reshape(nb, wide, lanes)
            block = jnp.sum(block, axis=1)
            for j in range(nb):
                den[j, t : t + 1, :] = block[j : j + 1]
        by_col = col[...]
        per = lanes // wide
        for j in range(nb):
            part = by_col[:, j // per * lanes : (j // per + 1) * lanes]
            turns = (-(j % per) * wide) % lanes
            part = pltpu.roll(part, turns, 1) if turns else part
            part = jnp.where(iota((nq, lanes), 1) < wide, part, 0.0)
            den[j] = (den[j] + part) * (2.0 ** (-SCALE))
            either(
                b == j,
                lambda: pltpu.make_async_copy(den.at[j], den_in.at[0, k_self], drecv1).start(),
                lambda: den1_copy(j, 0).start(),
            )
            den1_copy(j, 1).start()

    @pl.when(jnp.logical_not(computes))
    def _():
        pltpu.make_async_copy(ids3_in, ids3_in, irecv3).wait()
        for j in range(nx):
            passed_copy(j).wait_send()

    for j in range(nx - 2, nx):
        sent_stage(j)
    at_lane = iota((nq, lanes), 1)
    in_place = [at_lane // CAP == sub for sub in range(ns)]
    pltpu.make_async_copy(den_in, den_in, drecv1).wait()

    def ret_copy(v, t):
        return pltpu.make_async_remote_copy(
            src_ref=ret.at[v * na + t], dst_ref=ret_in.at[v * na + t],
            send_sem=dsend2.at[v, t], recv_sem=drecv2,
            device_id=(behind[t], left(v)), device_id_type=MESH,
        )

    for sub in range(ns):
        blocks = [jnp.zeros((nq, lanes), F32)] * 2
        for u in range(2):
            for k in range(nk):
                part = jnp.where(in_place[sub], den_in[u, k], 0.0)
                turns = ((u * nk + k - sub) * CAP) % lanes
                blocks[u] += pltpu.roll(part, turns, 1) if turns else part
        for v in range(2):
            for h in range(2):
                t = h * ns + sub
                at = 2 * v + h
                ret[v * na + t] = blocks[0][at : at + 1] + blocks[1][at + 4 : at + 5]
                if v + t > 0:
                    ret_copy(v, t).start()
                else:
                    pltpu.make_async_copy(ret.at[0], ret_in.at[0], drecv2).start()

    for i in range(1, na):
        ids1_copy(i).wait_send()
    for i in range(nb):
        @pl.when(b != i)
        def _():
            ids2_copy(i).wait_send()
    for j in range(1, nx):
        ids3_copy(j).wait_send()
    for q in range(2 * nx - 4, 2 * nx):
        forwarded(q)

    @pl.when(computes)
    def _():
        sib_ids_copy().wait_send()
        for q in range(nq):
            sib_rows_copy(q).wait_send()
        for i in range(nb):
            @pl.when(b != i)
            def _():
                den1_copy(i, 0).wait_send()

            den1_copy(i, 1).wait_send()

    chosen = (iota((lanes, rows), 0) == offset % 2 * na + step).astype(BF16)
    pltpu.make_async_copy(ret, ret_in, drecv2).wait()

    table = jnp.concatenate(
        [ret_in[m] for m in range(2 * na)] + [jnp.zeros((lanes - 2 * na, lanes), F32)], axis=0
    )
    table = table.T[: 2 * nk * CAP]
    high = table.astype(BF16)
    rest = table - high.astype(F32)
    mid = rest.astype(BF16)
    low = (rest - mid.astype(F32)).astype(BF16)
    picked = (
        jnp.dot(low, chosen, preferred_element_type=F32)
        + jnp.dot(mid, chosen, preferred_element_type=F32)
    ) + jnp.dot(high, chosen, preferred_element_type=F32)
    out_ref[...] = jnp.sum(
        jnp.where(iota((2 * nk * CAP, rows), 0) == offset // 2 * (nk * CAP) + lane, picked, 0.0),
        axis=0, keepdims=True,
    )

    for v in range(2):
        for t in range(na):
            if v + t > 0:
                ret_copy(v, t).wait_send()


def shards(n_tile, embeddings, cluster, home):
    n_shard = lax.axis_size("shard")
    na = next(n for n in range(1, n_shard + 1) if 2 * n * n == n_shard)
    nx = n_tile
    nk = 2 * na // nx
    rows, feat = embeddings.shape
    ns = na // 2
    nq = 2 * nx
    chunk = na * ns * CAP
    hf = feat // 2
    vmem = pltpu.VMEM
    dma = pltpu.SemaphoreType.DMA
    out = pl.pallas_call(
        functools.partial(kernel, na, nx),
        out_shape=jax.ShapeDtypeStruct((1, rows), F32),
        in_specs=[pl.BlockSpec(memory_space=pl.ANY)] * 3,
        out_specs=pl.BlockSpec(memory_space=pltpu.VMEM),
        scratch_shapes=[
            vmem((1, rows), I32),
            vmem((1, rows), I32),
            vmem((rows, feat), BF16),
            vmem((rows, feat), BF16),
            vmem((nq, ns, nk, 2 * CAP, hf), BF16),
            vmem((nq, ns, nk, 2 * CAP, hf), BF16),
            vmem((nq, na, ns, 2 * CAP, hf), BF16),
            vmem((nx, ns, 2 * CAP, hf), BF16),
            vmem((nq, chunk, feat), BF16),
            vmem((2, nq, chunk, feat), BF16),
            vmem((nq, chunk, 128), F32),
            vmem((nq, chunk), F32),
            vmem((8, chunk), F32),
            vmem((na, 1, 128), F32),
            vmem((na, 1, 128), F32),
            vmem((na, 128), F32),
            vmem((na, na, 128), F32),
            vmem((nx, na, na, 128), F32),
            vmem((nx, na, na, 128), F32),
            vmem((2, nq, 8, chunk), F32),
            vmem((2, nq, chunk, 128), F32),
            vmem((na, nq, 128), F32),
            vmem((2, nk, nq, 128), F32),
            vmem((2 * na, 1, 128), F32),
            vmem((2 * na, 1, 128), F32),
            dma((3,)),
            dma((nx, na)), dma((nq,)), dma((nq, nk)), dma((nq,)), dma((nq,)), dma((nq,)),
            dma((nx,)), dma((nx,)),
            dma((na,)), dma(()), dma((na,)), dma(()), dma((nx,)), dma(()), dma(()), dma(()),
            dma((na, 2)), dma(()), dma((2, na)), dma(()), pltpu.SemaphoreType.REGULAR,
        ],
        compiler_params=pltpu.CompilerParams(
            collective_id=0, has_side_effects=True, vmem_limit_bytes=48 * 2**20
        ),
    )(home.reshape(1, rows), cluster.reshape(1, rows), embeddings)
    return out.reshape(rows)


def solution(mesh):
    return jax.shard_map(
        functools.partial(shards, mesh.shape["tile"]),
        mesh=mesh,
        in_specs=(P(("shard", "tile"), None), P(("shard", "tile")), P(("shard", "tile"))),
        out_specs=P(("shard", "tile")),
        check_vma=False,
    )
```

```python
import functools

import jax
import jax.numpy as jnp
from jax import lax
from jax.experimental import pallas as pl
from jax.experimental.pallas import tpu as pltpu
from jax.sharding import PartitionSpec as P

F32 = jnp.float32
BF16 = jnp.bfloat16
I32 = jnp.int32
MESH = pl.DeviceIdType.MESH
CAP = 8
SCALE = 10.0 * 1.4426950408889634


def iota(shape, dim):
    return lax.broadcasted_iota(I32, shape, dim)


def nt_dot(left, right):
    return lax.dot_general(left, right, (((1,), (1,)), ((), ())), preferred_element_type=F32)


def kernel(
    na, nx, home_hbm, cluster_hbm, emb_hbm, out_ref,
    home_ref, cluster_ref, emb_ref, unit, out1, in1, in2, passing, sib_in, kept, acc, col, col_part, den_out, den_sib,
    ids1, ids1_in, ids2, ids2_in, ids3_in, ids_sib, key_ids, row_ids,
    den, den_in, ret, ret_in,
    load, send1, recv1, send2, recv2, send3, recv3, rsend, rrecv,
    isend1, irecv1, isend2, irecv2, isend3, irecv3, isend4, irecv4,
    dsend1, drecv1, dsend2, drecv2, dsend3, drecv3, entered,
):
    nb = na
    nk = 2 * nb // nx
    nj = nb // nx
    half = nx // 2
    rows, feat = emb_ref.shape
    hf = feat // 2
    ns = na // 2
    nq = 2 * nx
    chunk = nb * ns * CAP
    wide = ns * CAP
    lanes = 128

    loads = [
        pltpu.make_async_copy(src, dst, load.at[i])
        for i, (src, dst) in enumerate(
            [(home_hbm, home_ref), (cluster_hbm, cluster_ref), (emb_hbm, emb_ref)]
        )
    ]
    for copy in loads:
        copy.start()

    shard = lax.axis_index("shard")
    x = lax.axis_index("tile")
    core = lax.rem(shard, 2)
    y = lax.rem(lax.div(shard, 2), nb)
    z = lax.div(shard, 2 * nb)
    a = z + core * (y - z)
    b = y + core * (z - y)

    def on(a_to, b_to):
        z_to = a_to + core * (b_to - a_to)
        y_to = b_to + core * (a_to - b_to)
        return (z_to * nb + y_to) * 2 + core

    sibling = (shard + 1 - 2 * core, x)

    deltas = [0, 1, na - 1, na // 2]
    for far in range(2, na // 2):
        deltas += [far, na - far]

    ahead = [on(lax.rem(a + d, na), b) for d in deltas]
    behind = [on(lax.rem(a + na - d, na), b) for d in deltas]
    ring = [on(a, i) for i in range(nb)]
    b_to = [lax.rem(x - a - half * (k // nj) + nx + na * nx, nx) + nx * (k % nj) for k in range(nk)]
    owner = [on(a, b_to[k]) for k in range(nk)]
    stays = [b_to[k] == b for k in range(nk)]
    turn = lax.rem(x - a - b + 2 * na * nx, nx)
    computes = lax.rem(turn, half) == 0
    k_self = lax.div(turn, half) * nj + lax.div(b, nx)
    k_sib = lax.div(turn, half) * nj + lax.div(a, nx)

    opposite = [computes & (b_to[k] == lax.rem(b + nb // 2, nb)) for k in range(nk)]
    turned = 1 - 2 * lax.rem(b, 2)
    relay = on(a, lax.rem(b - turned + nb, nb))
    relay_from = lax.rem(b - turned + nb, nb)
    relay_to = on(a, lax.rem(b + (nb // 2 - 1) * turned + nb, nb))

    def either(same, local, remote):
        pl.when(same)(local)
        pl.when(jnp.logical_not(same))(remote)

    def right(j):
        return lax.rem(x + j, nx)

    def left(j):
        return lax.rem(x + nx - j, nx)

    barrier = pltpu.get_barrier_semaphore()

    def greet(device):
        pl.semaphore_signal(barrier, inc=1, device_id=device, device_id_type=MESH)

    for j in range(1, nx):
        greet((shard, right(j)))
    for t in range(1, na):
        greet((ahead[t], x))
    for i in range(nb):
        @pl.when(b != i)
        def _():
            greet((ring[i], x))
    greet(sibling)

    loads[0].wait()
    home = home_ref[...]
    named = iota((2 * na * nb, rows), 0) == home
    before = (iota((rows, rows), 0) < iota((rows, rows), 1)).astype(BF16)
    counts = jnp.dot(named.astype(BF16), before, preferred_element_type=F32)
    pos = jnp.sum(jnp.where(named, counts, 0.0), axis=0, keepdims=True).astype(I32)
    c_own = home % 2
    y_own = (home // 2) % nb
    z_own = home // (2 * nb)
    a_own = z_own + core * (y_own - z_own)
    b_own = y_own + core * (z_own - y_own)
    x_own = (a_own + b_own + half * c_own) % nx
    k_own = c_own * nj + b_own // nx
    distance = (a_own - a + na) % na
    step = jnp.zeros_like(distance)
    for t in range(1, na):
        step = jnp.where(distance == deltas[t], t, step)
    offset = (x_own - x + nx) % nx
    message = offset * na + step
    lane = k_own * CAP + pos
    slot = message * (nk * CAP) + lane
    wide_lane = offset * (nk * CAP) + lane

    loads[2].wait()
    values = emb_ref[...].astype(F32)
    unit[...] = (
        values * lax.rsqrt(jnp.sum(values * values, axis=1, keepdims=True) + 1e-06)
    ).astype(BF16)

    loads[1].wait()
    marks = (cluster_ref[...] + 1).astype(F32)
    in_step = (iota((na, rows), 0) == step).astype(BF16)
    in_lane = jnp.where(iota((lanes, rows), 0) == wide_lane, marks, 0.0)
    tags = nt_dot(in_step, in_lane.astype(BF16))
    for t in range(na):
        ids1[t] = tags[t : t + 1]

    def place(j, h):
        q = j * 2 + h
        size = ns * nk * CAP
        pick = (iota((size, rows), 0) + q * size == slot).astype(BF16)
        placed = jnp.dot(pick, unit[...], preferred_element_type=F32)
        placed = placed.reshape(ns * nk, CAP, feat)
        placed = jnp.concatenate([placed[:, :, :hf], placed[:, :, hf:]], axis=1).astype(BF16)
        out1[q] = placed.reshape(ns, nk, 2 * CAP, hf)

    for h in range(2):
        place(0, h)

    pl.semaphore_wait(barrier, nx - 1 + na - 1 + nb - 1 + 1)
    for j in range(1, nx):
        pl.semaphore_signal(
            entered, inc=1, device_id=(shard, right(j)), device_id_type=MESH
        )

    def ids1_copy(t):
        return pltpu.make_async_remote_copy(
            src_ref=ids1.at[t], dst_ref=ids1_in.at[t],
            send_sem=isend1.at[t], recv_sem=irecv1,
            device_id=(ahead[t], x), device_id_type=MESH,
        )

    def ids2_copy(i):
        return pltpu.make_async_remote_copy(
            src_ref=ids2, dst_ref=ids2_in.at[b],
            send_sem=isend2.at[i], recv_sem=irecv2,
            device_id=(ring[i], x), device_id_type=MESH,
        )

    def ids3_copy(j):
        return pltpu.make_async_remote_copy(
            src_ref=ids2_in, dst_ref=ids3_in.at[j],
            send_sem=isend3.at[j], recv_sem=irecv3,
            device_id=(shard, right(j)), device_id_type=MESH,
        )

    def out1_copy(j, t):
        q, sub = j * 2 + t // ns, t % ns
        return pltpu.make_async_remote_copy(
            src_ref=out1.at[q, sub], dst_ref=in1.at[q, sub],
            send_sem=send1.at[j, t], recv_sem=recv1.at[q],
            device_id=(ahead[t], right(j)), device_id_type=MESH,
        )

    def send_stage(j, first):
        for h in range(2):
            if not first:
                place(j, h)
            for t in range(h * ns, (h + 1) * ns):
                if first and t == 0:
                    pltpu.make_async_copy(out1.at[0, 0], in1.at[0, 0], recv1.at[0]).start()
                else:
                    out1_copy(j, t).start()

    def sent_stage(j):
        for t in range(na):
            if t > 0:
                out1_copy(j, t).wait_send()
            else:
                @pl.when(j > 0)
                def _():
                    out1_copy(j, t).wait_send()

    def rows2_copy(q, k):
        return pltpu.make_async_remote_copy(
            src_ref=in1.at[q, :, k], dst_ref=in2.at[q, b],
            send_sem=send2.at[q, k], recv_sem=recv2.at[q],
            device_id=(owner[k], x), device_id_type=MESH,
        )

    def forward(j, h):
        q = 2 * j + h
        pltpu.make_async_copy(in1.at[q], in1.at[q], recv1.at[q]).wait()
        for k in range(nk):
            def away(k=k):
                if h == 0:
                    rows2_copy(q, k).start()
                else:
                    either(
                        opposite[k],
                        lambda: relay_copy(j, k).start(),
                        lambda: rows2_copy(q, k).start(),
                    )

            either(
                stays[k],
                lambda: pltpu.make_async_copy(in1.at[q, :, k], in2.at[q, b], recv2.at[q]).start(),
                away,
            )

    def relay_copy(j, k):
        return pltpu.make_async_remote_copy(
            src_ref=in1.at[2 * j + 1, :, k], dst_ref=passing.at[j],
            send_sem=send2.at[2 * j + 1, k], recv_sem=rrecv.at[j],
            device_id=(relay, x), device_id_type=MESH,
        )

    def passed_copy(j):
        return pltpu.make_async_remote_copy(
            src_ref=passing.at[j], dst_ref=in2.at[2 * j + 1, relay_from],
            send_sem=rsend.at[j], recv_sem=recv2.at[2 * j + 1],
            device_id=(relay_to, x), device_id_type=MESH,
        )

    def forwarded(q):
        for k in range(nk):
            @pl.when(jnp.logical_not(stays[k]))
            def _():
                rows2_copy(q, k).wait_send()

    def sib_ids_copy():
        return pltpu.make_async_remote_copy(
            src_ref=ids3_in, dst_ref=ids_sib, send_sem=isend4, recv_sem=irecv4,
            device_id=sibling, device_id_type=MESH,
        )

    def sib_rows_copy(t):
        return pltpu.make_async_remote_copy(
            src_ref=kept.at[0, t], dst_ref=sib_in.at[t],
            send_sem=send3.at[t], recv_sem=recv3.at[t],
            device_id=sibling, device_id_type=MESH,
        )

    def spread_ids(source, side, k):
        def spread(q, carry):
            j, h = lax.div(q, 2), lax.rem(q, 2)
            block = jnp.concatenate(
                [source[j, i, pl.ds(h * ns, ns), :] for i in range(nb)], axis=0
            )
            block = jnp.broadcast_to(block[:, None, :], (nb * ns, CAP, lanes))
            here = iota((nb * ns, CAP, lanes), 1) + (j * nk + k) * CAP
            block = jnp.where(iota((nb * ns, CAP, lanes), 2) == here, block, 0.0)
            block = block.reshape(chunk, lanes)
            row_ids[side, q] = jnp.broadcast_to(
                jnp.sum(block, axis=1, keepdims=True), (chunk, lanes)
            )
            if side == 0:
                key_ids[q] = nt_dot(jnp.ones((8, lanes), BF16), block.astype(BF16))
            return carry

        lax.fori_loop(0, nq, spread, 0)

    def tile(size, side, t, last):
        left = kept[side, :size].reshape(size * chunk, feat)
        scores = nt_dot(left, kept[0, t])
        weights = jnp.exp2(scores * SCALE)
        theirs = key_ids[t, 0:1, :]
        sums = jnp.zeros((8, chunk), F32)
        for at in range(size):
            mine = row_ids[side, at]
            valid = jnp.where(at <= last, theirs, -1.0)
            matched = [
                jnp.where(
                    mine == valid[:, j : j + lanes],
                    weights[at * chunk : (at + 1) * chunk, j : j + lanes],
                    0.0,
                )
                for j in range(0, chunk, lanes)
            ]
            acc[side, at] += functools.reduce(jnp.add, matched)
            parts = [jnp.sum(m.reshape(chunk // 8, 8, lanes), axis=0) for m in matched]
            part = jnp.concatenate(parts, axis=1)
            sums += jnp.where(at < t, part, 0.0) if side == 0 else part
        col_part[...] += sums

    def strip(side, t, last):
        either(
            last < nq // 2,
            lambda: tile(nq // 2, side, t, last),
            lambda: either(
                last < nq // 4 * 3,
                lambda: tile(nq // 4 * 3, side, t, last),
                lambda: tile(nq, side, t, last),
            ),
        )

    def pair_sums(t, carry):
        pltpu.make_async_copy(in2.at[t], in2.at[t], recv2.at[t]).wait()
        block = in2[t].reshape(nb * ns, 2 * CAP, hf).astype(F32)
        block = jnp.concatenate([block[:, :CAP, :], block[:, CAP:, :]], axis=2)
        kept[0, t] = block.reshape(chunk, feat).astype(BF16)
        sib_rows_copy(t).start()

        col_part[...] = jnp.zeros_like(col_part)
        strip(0, t, t)
        sib_rows_copy(t).wait_recv()
        kept[1, t] = sib_in[t]
        strip(1, t, t - core)
        col[pl.ds(t, 1), :] = jnp.sum(col_part[...], axis=0, keepdims=True)
        return carry

    pltpu.make_async_copy(ids1.at[0], ids1_in.at[0], irecv1).start()
    for t in range(1, na):
        ids1_copy(t).start()
    send_stage(0, True)
    pltpu.make_async_copy(ids1, ids1_in, irecv1).wait()
    ids2[...] = jnp.concatenate([ids1_in[t] for t in range(na)], axis=0)
    for i in range(nb):
        either(
            b == i,
            lambda: pltpu.make_async_copy(ids2, ids2_in.at[b], irecv2).start(),
            lambda: ids2_copy(i).start(),
        )
    pl.semaphore_wait(entered, nx - 1)
    send_stage(1, False)

    def stage(j, carry):
        @pl.when(j < nx)
        def _():
            for h in range(2):
                @pl.when(j >= 2)
                def _():
                    forwarded(2 * j - 4 + h)

                forward(j, h)

            @pl.when(j == 0)
            def _():
                pltpu.make_async_copy(ids2_in, ids2_in, irecv2).wait()
                pltpu.make_async_copy(ids2_in, ids3_in.at[0], irecv3).start()
                for i in range(1, nx):
                    ids3_copy(i).start()

            @pl.when(j < nx - 2)
            def _():
                sent_stage(j)
                send_stage(j + 2, False)

            @pl.when(jnp.logical_not(computes))
            def _():
                pltpu.make_async_copy(passing.at[j], passing.at[j], rrecv.at[j]).wait()
                passed_copy(j).start()

        @pl.when(computes & (j == 1))
        def _():
            pltpu.make_async_copy(ids3_in, ids3_in, irecv3).wait()
            sib_ids_copy().start()
            spread_ids(ids3_in, 0, k_self)
            acc[...] = jnp.zeros_like(acc)
            sib_ids_copy().wait_recv()
            spread_ids(ids_sib, 1, k_sib)

        @pl.when(computes & (j > 0))
        def _():
            lax.fori_loop(2 * j - 2, 2 * j, pair_sums, 0)
        return carry

    lax.fori_loop(0, nx + 1, stage, 0)

    def sib_den_copy():
        return pltpu.make_async_remote_copy(
            src_ref=den_out, dst_ref=den_sib, send_sem=dsend3, recv_sem=drecv3,
            device_id=sibling, device_id_type=MESH,
        )

    def den1_copy(to, u):
        return pltpu.make_async_remote_copy(
            src_ref=den.at[to], dst_ref=den_in.at[u, k_self],
            send_sem=dsend1.at[to, u], recv_sem=drecv1,
            device_id=(ring[to], left(2 * u)), device_id_type=MESH,
        )

    @pl.when(computes)
    def _():
        same = iota((chunk, lanes), 1) == iota((chunk, lanes), 0) % wide
        for side, result in ((1, den_out), (0, den)):
            for t in range(nq):
                sums = jnp.sum(acc[side, t], axis=1, keepdims=True)
                block = jnp.where(same, sums, 0.0).reshape(nb, wide, lanes)
                block = jnp.sum(block, axis=1)
                for j in range(nb):
                    result[j, t : t + 1, :] = block[j : j + 1]
            if side == 1:
                sib_den_copy().start()
        by_col = col[...]
        per = lanes // wide
        sib_den_copy().wait_recv()
        for j in range(nb):
            part = by_col[:, j // per * lanes : (j // per + 1) * lanes]
            turns = (-(j % per) * wide) % lanes
            part = pltpu.roll(part, turns, 1) if turns else part
            part = jnp.where(iota((nq, lanes), 1) < wide, part, 0.0)
            den[j] = (den[j] + part + den_sib[j]) * (2.0 ** (-SCALE))
            either(
                b == j,
                lambda: pltpu.make_async_copy(den.at[j], den_in.at[0, k_self], drecv1).start(),
                lambda: den1_copy(j, 0).start(),
            )
            den1_copy(j, 1).start()

    @pl.when(jnp.logical_not(computes))
    def _():
        pltpu.make_async_copy(ids3_in, ids3_in, irecv3).wait()
        for j in range(nx):
            passed_copy(j).wait_send()

    for j in range(nx - 2, nx):
        sent_stage(j)
    at_lane = iota((nq, lanes), 1)
    in_place = [at_lane // CAP == sub for sub in range(ns)]
    pltpu.make_async_copy(den_in, den_in, drecv1).wait()

    def ret_copy(v, t):
        return pltpu.make_async_remote_copy(
            src_ref=ret.at[v * na + t], dst_ref=ret_in.at[v * na + t],
            send_sem=dsend2.at[v, t], recv_sem=drecv2,
            device_id=(behind[t], left(v)), device_id_type=MESH,
        )

    for sub in range(ns):
        blocks = [jnp.zeros((nq, lanes), F32)] * 2
        for u in range(2):
            for k in range(nk):
                part = jnp.where(in_place[sub], den_in[u, k], 0.0)
                turns = ((u * nk + k - sub) * CAP) % lanes
                blocks[u] += pltpu.roll(part, turns, 1) if turns else part
        for v in range(2):
            for h in range(2):
                t = h * ns + sub
                at = 2 * v + h
                ret[v * na + t] = blocks[0][at : at + 1] + blocks[1][at + 4 : at + 5]
                if v + t > 0:
                    ret_copy(v, t).start()
                else:
                    pltpu.make_async_copy(ret.at[0], ret_in.at[0], drecv2).start()

    for i in range(1, na):
        ids1_copy(i).wait_send()
    for i in range(nb):
        @pl.when(b != i)
        def _():
            ids2_copy(i).wait_send()
    for j in range(1, nx):
        ids3_copy(j).wait_send()
    for q in range(2 * nx - 4, 2 * nx):
        forwarded(q)

    @pl.when(computes)
    def _():
        sib_ids_copy().wait_send()
        sib_den_copy().wait_send()
        for q in range(nq):
            sib_rows_copy(q).wait_send()
        for i in range(nb):
            @pl.when(b != i)
            def _():
                den1_copy(i, 0).wait_send()

            den1_copy(i, 1).wait_send()

    chosen = (iota((lanes, rows), 0) == offset % 2 * na + step).astype(BF16)
    pltpu.make_async_copy(ret, ret_in, drecv2).wait()

    table = jnp.concatenate(
        [ret_in[m] for m in range(2 * na)] + [jnp.zeros((lanes - 2 * na, lanes), F32)], axis=0
    )
    table = table.T[: 2 * nk * CAP]
    high = table.astype(BF16)
    rest = table - high.astype(F32)
    mid = rest.astype(BF16)
    low = (rest - mid.astype(F32)).astype(BF16)
    picked = (
        jnp.dot(low, chosen, preferred_element_type=F32)
        + jnp.dot(mid, chosen, preferred_element_type=F32)
    ) + jnp.dot(high, chosen, preferred_element_type=F32)
    out_ref[...] = jnp.sum(
        jnp.where(iota((2 * nk * CAP, rows), 0) == offset // 2 * (nk * CAP) + lane, picked, 0.0),
        axis=0, keepdims=True,
    )

    for v in range(2):
        for t in range(na):
            if v + t > 0:
                ret_copy(v, t).wait_send()


def shards(n_tile, embeddings, cluster, home):
    n_shard = lax.axis_size("shard")
    na = next(n for n in range(1, n_shard + 1) if 2 * n * n == n_shard)
    nx = n_tile
    nk = 2 * na // nx
    rows, feat = embeddings.shape
    ns = na // 2
    nq = 2 * nx
    chunk = na * ns * CAP
    hf = feat // 2
    vmem = pltpu.VMEM
    dma = pltpu.SemaphoreType.DMA
    out = pl.pallas_call(
        functools.partial(kernel, na, nx),
        out_shape=jax.ShapeDtypeStruct((1, rows), F32),
        in_specs=[pl.BlockSpec(memory_space=pl.ANY)] * 3,
        out_specs=pl.BlockSpec(memory_space=pltpu.VMEM),
        scratch_shapes=[
            vmem((1, rows), I32),
            vmem((1, rows), I32),
            vmem((rows, feat), BF16),
            vmem((rows, feat), BF16),
            vmem((nq, ns, nk, 2 * CAP, hf), BF16),
            vmem((nq, ns, nk, 2 * CAP, hf), BF16),
            vmem((nq, na, ns, 2 * CAP, hf), BF16),
            vmem((nx, ns, 2 * CAP, hf), BF16),
            vmem((nq, chunk, feat), BF16),
            vmem((2, nq, chunk, feat), BF16),
            vmem((2, nq, chunk, 128), F32),
            vmem((nq, chunk), F32),
            vmem((8, chunk), F32),
            vmem((na, nq, 128), F32),
            vmem((na, nq, 128), F32),
            vmem((na, 1, 128), F32),
            vmem((na, 1, 128), F32),
            vmem((na, 128), F32),
            vmem((na, na, 128), F32),
            vmem((nx, na, na, 128), F32),
            vmem((nx, na, na, 128), F32),
            vmem((nq, 8, chunk), F32),
            vmem((2, nq, chunk, 128), F32),
            vmem((na, nq, 128), F32),
            vmem((2, nk, nq, 128), F32),
            vmem((2 * na, 1, 128), F32),
            vmem((2 * na, 1, 128), F32),
            dma((3,)),
            dma((nx, na)), dma((nq,)), dma((nq, nk)), dma((nq,)), dma((nq,)), dma((nq,)),
            dma((nx,)), dma((nx,)),
            dma((na,)), dma(()), dma((na,)), dma(()), dma((nx,)), dma(()), dma(()), dma(()),
            dma((na, 2)), dma(()), dma((2, na)), dma(()), dma(()), dma(()),
            pltpu.SemaphoreType.REGULAR,
        ],
        compiler_params=pltpu.CompilerParams(
            collective_id=0, has_side_effects=True, vmem_limit_bytes=48 * 2**20
        ),
    )(home.reshape(1, rows), cluster.reshape(1, rows), embeddings)
    return out.reshape(rows)


def solution(mesh):
    return jax.shard_map(
        functools.partial(shards, mesh.shape["tile"]),
        mesh=mesh,
        in_specs=(P(("shard", "tile"), None), P(("shard", "tile")), P(("shard", "tile"))),
        out_specs=P(("shard", "tile")),
        check_vma=False,
    )
```

```python
import functools

import jax
import jax.numpy as jnp
from jax import lax
from jax.experimental import pallas as pl
from jax.experimental.pallas import tpu as pltpu
from jax.sharding import PartitionSpec as P

F32 = jnp.float32
BF16 = jnp.bfloat16
I32 = jnp.int32
MESH = pl.DeviceIdType.MESH
CAP = 8
SCALE = 10.0 * 1.4426950408889634


def iota(shape, dim):
    return lax.broadcasted_iota(I32, shape, dim)


def nt_dot(left, right):
    return lax.dot_general(left, right, (((1,), (1,)), ((), ())), preferred_element_type=F32)


def kernel(
    na, nx, home_hbm, cluster_hbm, emb_hbm, out_ref,
    home_ref, cluster_ref, emb_ref, unit, out1, in1, in2, passing, sib_in, kept, acc, col, col_part, den_out, den_sib,
    ids1, ids1_in, ids2, ids2_in, ids3_in, ids_sib, key_ids, row_ids,
    den, den_in, ret, ret_in,
    load, send1, recv1, send2, recv2, send3, recv3, rsend, rrecv,
    isend1, irecv1, isend2, irecv2, isend3, irecv3, isend4, irecv4,
    dsend1, drecv1, dsend2, drecv2, dsend3, drecv3, entered,
):
    nb = na
    nk = 2 * nb // nx
    nj = nb // nx
    half = nx // 2
    rows, feat = emb_ref.shape
    hf = feat // 2
    ns = na // 2
    nq = 2 * nx
    chunk = nb * ns * CAP
    wide = ns * CAP
    lanes = 128

    loads = [
        pltpu.make_async_copy(src, dst, load.at[i])
        for i, (src, dst) in enumerate(
            [(home_hbm, home_ref), (cluster_hbm, cluster_ref), (emb_hbm, emb_ref)]
        )
    ]
    for copy in loads:
        copy.start()

    shard = lax.axis_index("shard")
    x = lax.axis_index("tile")
    core = lax.rem(shard, 2)
    y = lax.rem(lax.div(shard, 2), nb)
    z = lax.div(shard, 2 * nb)
    a = z + core * (y - z)
    b = y + core * (z - y)

    def on(a_to, b_to):
        z_to = a_to + core * (b_to - a_to)
        y_to = b_to + core * (a_to - b_to)
        return (z_to * nb + y_to) * 2 + core

    sibling = (shard + 1 - 2 * core, x)

    deltas = [0, 1, na - 1, na // 2]
    for far in range(2, na // 2):
        deltas += [far, na - far]

    ahead = [on(lax.rem(a + d, na), b) for d in deltas]
    behind = [on(lax.rem(a + na - d, na), b) for d in deltas]
    ring = [on(a, i) for i in range(nb)]
    b_to = [lax.rem(x - a - half * (k // nj) + nx + na * nx, nx) + nx * (k % nj) for k in range(nk)]
    owner = [on(a, b_to[k]) for k in range(nk)]
    stays = [b_to[k] == b for k in range(nk)]
    turn = lax.rem(x - a - b + 2 * na * nx, nx)
    computes = lax.rem(turn, half) == 0
    k_self = lax.div(turn, half) * nj + lax.div(b, nx)
    k_sib = lax.div(turn, half) * nj + lax.div(a, nx)

    opposite = [computes & (b_to[k] == lax.rem(b + nb // 2, nb)) for k in range(nk)]
    turned = 1 - 2 * lax.rem(b, 2)
    relay = on(a, lax.rem(b - turned + nb, nb))
    relay_from = lax.rem(b - turned + nb, nb)
    relay_to = on(a, lax.rem(b + (nb // 2 - 1) * turned + nb, nb))

    def either(same, local, remote):
        pl.when(same)(local)
        pl.when(jnp.logical_not(same))(remote)

    def right(j):
        return lax.rem(x + j, nx)

    def left(j):
        return lax.rem(x + nx - j, nx)

    barrier = pltpu.get_barrier_semaphore()

    def greet(device):
        pl.semaphore_signal(barrier, inc=1, device_id=device, device_id_type=MESH)

    for j in range(1, nx):
        greet((shard, right(j)))
    for t in range(1, na):
        greet((ahead[t], x))
    for i in range(nb):
        @pl.when(b != i)
        def _():
            greet((ring[i], x))
    greet(sibling)

    loads[0].wait()
    home = home_ref[...]
    named = iota((2 * na * nb, rows), 0) == home
    before = (iota((rows, rows), 0) < iota((rows, rows), 1)).astype(BF16)
    counts = jnp.dot(named.astype(BF16), before, preferred_element_type=F32)
    pos = jnp.sum(jnp.where(named, counts, 0.0), axis=0, keepdims=True).astype(I32)
    c_own = home % 2
    y_own = (home // 2) % nb
    z_own = home // (2 * nb)
    a_own = z_own + core * (y_own - z_own)
    b_own = y_own + core * (z_own - y_own)
    x_own = (a_own + b_own + half * c_own) % nx
    k_own = c_own * nj + b_own // nx
    distance = (a_own - a + na) % na
    step = jnp.zeros_like(distance)
    for t in range(1, na):
        step = jnp.where(distance == deltas[t], t, step)
    offset = (x_own - x + nx) % nx
    message = offset * na + step
    lane = k_own * CAP + pos
    slot = message * (nk * CAP) + lane
    wide_lane = offset * (nk * CAP) + lane

    loads[2].wait()
    values = emb_ref[...].astype(F32)
    unit[...] = (
        values * lax.rsqrt(jnp.sum(values * values, axis=1, keepdims=True) + 1e-06)
    ).astype(BF16)

    loads[1].wait()
    marks = (cluster_ref[...] + 1).astype(F32)
    in_step = (iota((na, rows), 0) == step).astype(BF16)
    in_lane = jnp.where(iota((lanes, rows), 0) == wide_lane, marks, 0.0)
    tags = nt_dot(in_step, in_lane.astype(BF16))
    for t in range(na):
        ids1[t] = tags[t : t + 1]

    def place(j, h):
        q = j * 2 + h
        size = ns * nk * CAP
        pick = (iota((size, rows), 0) + q * size == slot).astype(BF16)
        placed = jnp.dot(pick, unit[...], preferred_element_type=F32)
        placed = placed.reshape(ns * nk, CAP, feat)
        placed = jnp.concatenate([placed[:, :, :hf], placed[:, :, hf:]], axis=1).astype(BF16)
        out1[q] = placed.reshape(ns, nk, 2 * CAP, hf)

    for h in range(2):
        place(0, h)

    pl.semaphore_wait(barrier, nx - 1 + na - 1 + nb - 1 + 1)
    for j in range(1, nx):
        pl.semaphore_signal(
            entered, inc=1, device_id=(shard, right(j)), device_id_type=MESH
        )

    def ids1_copy(t):
        return pltpu.make_async_remote_copy(
            src_ref=ids1.at[t], dst_ref=ids1_in.at[t],
            send_sem=isend1.at[t], recv_sem=irecv1,
            device_id=(ahead[t], x), device_id_type=MESH,
        )

    def ids2_copy(i):
        return pltpu.make_async_remote_copy(
            src_ref=ids2, dst_ref=ids2_in.at[b],
            send_sem=isend2.at[i], recv_sem=irecv2,
            device_id=(ring[i], x), device_id_type=MESH,
        )

    def ids3_copy(j):
        return pltpu.make_async_remote_copy(
            src_ref=ids2_in, dst_ref=ids3_in.at[j],
            send_sem=isend3.at[j], recv_sem=irecv3,
            device_id=(shard, right(j)), device_id_type=MESH,
        )

    def out1_copy(j, t):
        q, sub = j * 2 + t // ns, t % ns
        return pltpu.make_async_remote_copy(
            src_ref=out1.at[q, sub], dst_ref=in1.at[q, sub],
            send_sem=send1.at[j, t], recv_sem=recv1.at[q],
            device_id=(ahead[t], right(j)), device_id_type=MESH,
        )

    def send_stage(j, first):
        for h in range(2):
            if not first:
                place(j, h)
            for t in range(h * ns, (h + 1) * ns):
                if first and t == 0:
                    pltpu.make_async_copy(out1.at[0, 0], in1.at[0, 0], recv1.at[0]).start()
                else:
                    out1_copy(j, t).start()

    def sent_stage(j):
        for t in range(na):
            if t > 0:
                out1_copy(j, t).wait_send()
            else:
                @pl.when(j > 0)
                def _():
                    out1_copy(j, t).wait_send()

    def rows2_copy(q, k):
        return pltpu.make_async_remote_copy(
            src_ref=in1.at[q, :, k], dst_ref=in2.at[q, b],
            send_sem=send2.at[q, k], recv_sem=recv2.at[q],
            device_id=(owner[k], x), device_id_type=MESH,
        )

    def forward(j, h):
        q = 2 * j + h
        pltpu.make_async_copy(in1.at[q], in1.at[q], recv1.at[q]).wait()
        for k in range(nk):
            def away(k=k):
                if h == 0:
                    rows2_copy(q, k).start()
                else:
                    either(
                        opposite[k],
                        lambda: relay_copy(j, k).start(),
                        lambda: rows2_copy(q, k).start(),
                    )

            either(
                stays[k],
                lambda: pltpu.make_async_copy(in1.at[q, :, k], in2.at[q, b], recv2.at[q]).start(),
                away,
            )

    def relay_copy(j, k):
        return pltpu.make_async_remote_copy(
            src_ref=in1.at[2 * j + 1, :, k], dst_ref=passing.at[j],
            send_sem=send2.at[2 * j + 1, k], recv_sem=rrecv.at[j],
            device_id=(relay, x), device_id_type=MESH,
        )

    def passed_copy(j):
        return pltpu.make_async_remote_copy(
            src_ref=passing.at[j], dst_ref=in2.at[2 * j + 1, relay_from],
            send_sem=rsend.at[j], recv_sem=recv2.at[2 * j + 1],
            device_id=(relay_to, x), device_id_type=MESH,
        )

    def forwarded(q):
        for k in range(nk):
            @pl.when(jnp.logical_not(stays[k]))
            def _():
                rows2_copy(q, k).wait_send()

    def sib_ids_copy():
        return pltpu.make_async_remote_copy(
            src_ref=ids3_in, dst_ref=ids_sib, send_sem=isend4, recv_sem=irecv4,
            device_id=sibling, device_id_type=MESH,
        )

    def sib_rows_copy(t):
        return pltpu.make_async_remote_copy(
            src_ref=kept.at[0, t], dst_ref=sib_in.at[t],
            send_sem=send3.at[t], recv_sem=recv3.at[t],
            device_id=sibling, device_id_type=MESH,
        )

    def spread_ids(source, side, k):
        def spread(q, carry):
            j, h = lax.div(q, 2), lax.rem(q, 2)
            block = jnp.concatenate(
                [source[j, i, pl.ds(h * ns, ns), :] for i in range(nb)], axis=0
            )
            block = jnp.broadcast_to(block[:, None, :], (nb * ns, CAP, lanes))
            here = iota((nb * ns, CAP, lanes), 1) + (j * nk + k) * CAP
            block = jnp.where(iota((nb * ns, CAP, lanes), 2) == here, block, 0.0)
            block = block.reshape(chunk, lanes)
            row_ids[side, q] = jnp.broadcast_to(
                jnp.sum(block, axis=1, keepdims=True), (chunk, lanes)
            )
            if side == 0:
                key_ids[q] = nt_dot(jnp.ones((8, lanes), BF16), block.astype(BF16))
            return carry

        lax.fori_loop(0, nq, spread, 0)

    def tile(size, side, t, last):
        left = kept[side, :size].reshape(size * chunk, feat)
        scores = nt_dot(left, kept[0, t])
        weights = jnp.exp2(scores * SCALE)
        theirs = key_ids[t, 0:1, :]
        sums = jnp.zeros((8, chunk), F32)
        for at in range(size):
            mine = row_ids[side, at]
            valid = jnp.where(at <= last, theirs, -1.0)
            matched = [
                jnp.where(
                    mine == valid[:, j : j + lanes],
                    weights[at * chunk : (at + 1) * chunk, j : j + lanes],
                    0.0,
                )
                for j in range(0, chunk, lanes)
            ]
            acc[side, at] += functools.reduce(jnp.add, matched)
            parts = [jnp.sum(m.reshape(chunk // 8, 8, lanes), axis=0) for m in matched]
            part = jnp.concatenate(parts, axis=1)
            sums += jnp.where(at < t, part, 0.0) if side == 0 else part
        col_part[...] += sums

    def strip(side, t, last):
        for size in range(2, nq + 1, 2):
            @pl.when((last >= size - 2) & (last < size))
            def _():
                tile(size, side, t, last)

    def pair_sums(t, carry):
        pltpu.make_async_copy(in2.at[t], in2.at[t], recv2.at[t]).wait()
        block = in2[t].reshape(nb * ns, 2 * CAP, hf).astype(F32)
        block = jnp.concatenate([block[:, :CAP, :], block[:, CAP:, :]], axis=2)
        kept[0, t] = block.reshape(chunk, feat).astype(BF16)
        sib_rows_copy(t).start()

        col_part[...] = jnp.zeros_like(col_part)
        strip(0, t, t)
        sib_rows_copy(t).wait_recv()
        kept[1, t] = sib_in[t]
        strip(1, t, t - core)
        col[pl.ds(t, 1), :] = jnp.sum(col_part[...], axis=0, keepdims=True)
        return carry

    pltpu.make_async_copy(ids1.at[0], ids1_in.at[0], irecv1).start()
    for t in range(1, na):
        ids1_copy(t).start()
    send_stage(0, True)
    pltpu.make_async_copy(ids1, ids1_in, irecv1).wait()
    ids2[...] = jnp.concatenate([ids1_in[t] for t in range(na)], axis=0)
    for i in range(nb):
        either(
            b == i,
            lambda: pltpu.make_async_copy(ids2, ids2_in.at[b], irecv2).start(),
            lambda: ids2_copy(i).start(),
        )
    pl.semaphore_wait(entered, nx - 1)
    send_stage(1, False)

    def stage(j, carry):
        @pl.when(j < nx)
        def _():
            for h in range(2):
                @pl.when(j >= 2)
                def _():
                    forwarded(2 * j - 4 + h)

                forward(j, h)

            @pl.when(j == 0)
            def _():
                pltpu.make_async_copy(ids2_in, ids2_in, irecv2).wait()
                pltpu.make_async_copy(ids2_in, ids3_in.at[0], irecv3).start()
                for i in range(1, nx):
                    ids3_copy(i).start()

            @pl.when(j < nx - 2)
            def _():
                sent_stage(j)
                send_stage(j + 2, False)

            @pl.when(jnp.logical_not(computes))
            def _():
                pltpu.make_async_copy(passing.at[j], passing.at[j], rrecv.at[j]).wait()
                passed_copy(j).start()

        @pl.when(computes & (j == 1))
        def _():
            pltpu.make_async_copy(ids3_in, ids3_in, irecv3).wait()
            sib_ids_copy().start()
            spread_ids(ids3_in, 0, k_self)
            acc[...] = jnp.zeros_like(acc)
            sib_ids_copy().wait_recv()
            spread_ids(ids_sib, 1, k_sib)

        @pl.when(computes & (j > 0))
        def _():
            lax.fori_loop(2 * j - 2, 2 * j, pair_sums, 0)
        return carry

    lax.fori_loop(0, nx + 1, stage, 0)

    def sib_den_copy():
        return pltpu.make_async_remote_copy(
            src_ref=den_out, dst_ref=den_sib, send_sem=dsend3, recv_sem=drecv3,
            device_id=sibling, device_id_type=MESH,
        )

    def den1_copy(to, u):
        return pltpu.make_async_remote_copy(
            src_ref=den.at[to], dst_ref=den_in.at[u, k_self],
            send_sem=dsend1.at[to, u], recv_sem=drecv1,
            device_id=(ring[to], left(2 * u)), device_id_type=MESH,
        )

    @pl.when(computes)
    def _():
        same = iota((chunk, lanes), 1) == iota((chunk, lanes), 0) % wide
        for side, result in ((1, den_out), (0, den)):
            for t in range(nq):
                sums = jnp.sum(acc[side, t], axis=1, keepdims=True)
                block = jnp.where(same, sums, 0.0).reshape(nb, wide, lanes)
                block = jnp.sum(block, axis=1)
                for j in range(nb):
                    result[j, t : t + 1, :] = block[j : j + 1]
            if side == 1:
                sib_den_copy().start()
        by_col = col[...]
        per = lanes // wide
        sib_den_copy().wait_recv()
        for j in range(nb):
            part = by_col[:, j // per * lanes : (j // per + 1) * lanes]
            turns = (-(j % per) * wide) % lanes
            part = pltpu.roll(part, turns, 1) if turns else part
            part = jnp.where(iota((nq, lanes), 1) < wide, part, 0.0)
            den[j] = (den[j] + part + den_sib[j]) * (2.0 ** (-SCALE))
            either(
                b == j,
                lambda: pltpu.make_async_copy(den.at[j], den_in.at[0, k_self], drecv1).start(),
                lambda: den1_copy(j, 0).start(),
            )
            den1_copy(j, 1).start()

    @pl.when(jnp.logical_not(computes))
    def _():
        pltpu.make_async_copy(ids3_in, ids3_in, irecv3).wait()
        for j in range(nx):
            passed_copy(j).wait_send()

    for j in range(nx - 2, nx):
        sent_stage(j)
    at_lane = iota((nq, lanes), 1)
    in_place = [at_lane // CAP == sub for sub in range(ns)]
    pltpu.make_async_copy(den_in, den_in, drecv1).wait()

    def ret_copy(v, t):
        return pltpu.make_async_remote_copy(
            src_ref=ret.at[v * na + t], dst_ref=ret_in.at[v * na + t],
            send_sem=dsend2.at[v, t], recv_sem=drecv2,
            device_id=(behind[t], left(v)), device_id_type=MESH,
        )

    for sub in range(ns):
        blocks = [jnp.zeros((nq, lanes), F32)] * 2
        for u in range(2):
            for k in range(nk):
                part = jnp.where(in_place[sub], den_in[u, k], 0.0)
                turns = ((u * nk + k - sub) * CAP) % lanes
                blocks[u] += pltpu.roll(part, turns, 1) if turns else part
        for v in range(2):
            for h in range(2):
                t = h * ns + sub
                at = 2 * v + h
                ret[v * na + t] = blocks[0][at : at + 1] + blocks[1][at + 4 : at + 5]
                if v + t > 0:
                    ret_copy(v, t).start()
                else:
                    pltpu.make_async_copy(ret.at[0], ret_in.at[0], drecv2).start()

    for i in range(1, na):
        ids1_copy(i).wait_send()
    for i in range(nb):
        @pl.when(b != i)
        def _():
            ids2_copy(i).wait_send()
    for j in range(1, nx):
        ids3_copy(j).wait_send()
    for q in range(2 * nx - 4, 2 * nx):
        forwarded(q)

    @pl.when(computes)
    def _():
        sib_ids_copy().wait_send()
        sib_den_copy().wait_send()
        for q in range(nq):
            sib_rows_copy(q).wait_send()
        for i in range(nb):
            @pl.when(b != i)
            def _():
                den1_copy(i, 0).wait_send()

            den1_copy(i, 1).wait_send()

    chosen = (iota((lanes, rows), 0) == offset % 2 * na + step).astype(BF16)
    pltpu.make_async_copy(ret, ret_in, drecv2).wait()

    table = jnp.concatenate(
        [ret_in[m] for m in range(2 * na)] + [jnp.zeros((lanes - 2 * na, lanes), F32)], axis=0
    )
    table = table.T[: 2 * nk * CAP]
    high = table.astype(BF16)
    rest = table - high.astype(F32)
    mid = rest.astype(BF16)
    low = (rest - mid.astype(F32)).astype(BF16)
    picked = (
        jnp.dot(low, chosen, preferred_element_type=F32)
        + jnp.dot(mid, chosen, preferred_element_type=F32)
    ) + jnp.dot(high, chosen, preferred_element_type=F32)
    out_ref[...] = jnp.sum(
        jnp.where(iota((2 * nk * CAP, rows), 0) == offset // 2 * (nk * CAP) + lane, picked, 0.0),
        axis=0, keepdims=True,
    )

    for v in range(2):
        for t in range(na):
            if v + t > 0:
                ret_copy(v, t).wait_send()


def shards(n_tile, embeddings, cluster, home):
    n_shard = lax.axis_size("shard")
    na = next(n for n in range(1, n_shard + 1) if 2 * n * n == n_shard)
    nx = n_tile
    nk = 2 * na // nx
    rows, feat = embeddings.shape
    ns = na // 2
    nq = 2 * nx
    chunk = na * ns * CAP
    hf = feat // 2
    vmem = pltpu.VMEM
    dma = pltpu.SemaphoreType.DMA
    out = pl.pallas_call(
        functools.partial(kernel, na, nx),
        out_shape=jax.ShapeDtypeStruct((1, rows), F32),
        in_specs=[pl.BlockSpec(memory_space=pl.ANY)] * 3,
        out_specs=pl.BlockSpec(memory_space=pltpu.VMEM),
        scratch_shapes=[
            vmem((1, rows), I32),
            vmem((1, rows), I32),
            vmem((rows, feat), BF16),
            vmem((rows, feat), BF16),
            vmem((nq, ns, nk, 2 * CAP, hf), BF16),
            vmem((nq, ns, nk, 2 * CAP, hf), BF16),
            vmem((nq, na, ns, 2 * CAP, hf), BF16),
            vmem((nx, ns, 2 * CAP, hf), BF16),
            vmem((nq, chunk, feat), BF16),
            vmem((2, nq, chunk, feat), BF16),
            vmem((2, nq, chunk, 128), F32),
            vmem((nq, chunk), F32),
            vmem((8, chunk), F32),
            vmem((na, nq, 128), F32),
            vmem((na, nq, 128), F32),
            vmem((na, 1, 128), F32),
            vmem((na, 1, 128), F32),
            vmem((na, 128), F32),
            vmem((na, na, 128), F32),
            vmem((nx, na, na, 128), F32),
            vmem((nx, na, na, 128), F32),
            vmem((nq, 8, chunk), F32),
            vmem((2, nq, chunk, 128), F32),
            vmem((na, nq, 128), F32),
            vmem((2, nk, nq, 128), F32),
            vmem((2 * na, 1, 128), F32),
            vmem((2 * na, 1, 128), F32),
            dma((3,)),
            dma((nx, na)), dma((nq,)), dma((nq, nk)), dma((nq,)), dma((nq,)), dma((nq,)),
            dma((nx,)), dma((nx,)),
            dma((na,)), dma(()), dma((na,)), dma(()), dma((nx,)), dma(()), dma(()), dma(()),
            dma((na, 2)), dma(()), dma((2, na)), dma(()), dma(()), dma(()),
            pltpu.SemaphoreType.REGULAR,
        ],
        compiler_params=pltpu.CompilerParams(
            collective_id=0, has_side_effects=True, vmem_limit_bytes=48 * 2**20
        ),
    )(home.reshape(1, rows), cluster.reshape(1, rows), embeddings)
    return out.reshape(rows)


def solution(mesh):
    return jax.shard_map(
        functools.partial(shards, mesh.shape["tile"]),
        mesh=mesh,
        in_specs=(P(("shard", "tile"), None), P(("shard", "tile")), P(("shard", "tile"))),
        out_specs=P(("shard", "tile")),
        check_vma=False,
    )
```
